128 devices in a mesh: dp: 8 (over x, core), ctx: 16 (over z, y).
Axes of the slice: x: 4, y: 4, z: 4, core: 2. Of those that a mesh axis runs over, the one named last changes fastest.
Arguments:
- normed: bfloat16 [8, 2048, 4096], P('dp', 'ctx'), may hold values from -6 to 6
- queries: bfloat16 [8, 2048, 2048], P('dp', 'ctx'), may hold values from -80 to 80
- cotangent: bfloat16 [8, 2048, 2048], P('dp', 'ctx'), may hold values from -6 to 6
- lengths: int32 [8, 8], P('dp'), may hold values from 1 to 1024, 2048 in all within a row
- balanced_slot: int32 [8, 2048], P('dp', 'ctx'), may hold values from 0 to 2047, as said below
- kv_weight: bfloat16 [4096, 1024], replicated, may hold values from -0.09375 to 0.09375
Outputs:
- attn_out: bfloat16 [8, 2048, 2048], P('dp', 'ctx')
- q_grad: bfloat16 [8, 2048, 2048], P('dp', 'ctx')
- input_grad: bfloat16 [8, 2048, 4096], P('dp', 'ctx')
- weight_grad: float32 [4096, 1024], P(('dp', 'ctx'))
The draws below stay inside these ranges and needn't reach their ends.
Inputs may be any that keep to these rules, and one draw needn't show every extreme that they name: `balanced_slot`: each row is a permutation of the positions. A token of even block s (positions s*128 to (s+1)*128 - 1) goes to balanced block slot // 128, at row s*8 + slot mod 8 of that block; every even block sends exactly 8 tokens to every balanced block.
All inputs are finite; a program needn't handle non-finite values.
Results may differ from the reference program's by a relative error of at most 0.023.
The reference program's roundings to bfloat16 on the way (of `kv_rows`, `grad_even`, `prob_b16`, `grad_scores` and `kv_grad`) count: a program that leaves them out, or rounds other values in their place, can miss the bound.
Values may be sent and summed in bfloat16 or wider, within the bound.
No kernel may reach another device: no remote copies, remote signals or barrier semaphores. Data moves between devices by JAX's collectives and lax.ppermute only.
A program may use at most 128 MiB of HBM per device.

```python
import math
import jax
import jax.numpy as jnp
import numpy as np
from jax import lax

D = 4096
HD = 128
KVH = 4
GROUP = 4
NDOC = 8
TOK_DEV = 128
QW = 2048
KVW = 512
SEQ = 2048
SHARE = 8
LMAX = 1024
BATCHES = 8


def draw_queries(key, part):
    key = jax.random.fold_in(key, 11)
    base_key, scale_key = jax.random.split(key)
    values = jnp.clip(jax.random.normal(base_key, (BATCHES, SEQ, QW), jnp.float32), -6.0, 6.0)
    scales = jnp.exp(jax.random.uniform(scale_key, (BATCHES, SEQ, 1), jnp.float32, 0.0, math.log(4.0)))
    return (values * scales).astype(jnp.bfloat16)


def draw_balanced_slot(key, part):
    key = jax.random.fold_in(key, 7)
    blocks = SEQ // TOK_DEV
    keys = jax.random.split(key, BATCHES * blocks)
    perms = jax.vmap(lambda single: jax.random.permutation(single, TOK_DEV))(keys)
    perms = perms.reshape(BATCHES, blocks, TOK_DEV).astype(jnp.int32)
    source = jnp.arange(blocks, dtype=jnp.int32)[None, :, None]
    slots = perms // SHARE * TOK_DEV + source * SHARE + perms % SHARE
    return slots.reshape(BATCHES, SEQ).astype(jnp.int32)


def steps_of(own_key, extent, pieces, smallest, largest):
    level, own = 1.0, jax.random.fold_in(own_key, 6)
    for position, shards_of in pieces:
        heights = jnp.exp(jax.random.uniform(jax.random.fold_in(own, position), (shards_of,), jnp.float32, smallest / len(pieces), largest / len(pieces)))
        level = level * jnp.repeat(heights, extent[position] // shards_of).reshape([-1 if axis == position else 1 for axis in range(len(extent))])
    return level


def profile(number_of, total, most, slope):
    weights = [(1 << 20) // math.isqrt(rank ** slope) + 1 for rank in range(2, number_of + 1)]
    spare, counts = total - most - (number_of - 1), [1] * (number_of - 1)
    while spare > 0:
        free = [i for i in range(number_of - 1) if counts[i] < most]
        mass, left = sum([weights[i] for i in free]), spare
        for i in free:
            extra = min(most - counts[i], max(1, left * weights[i] // mass), spare)
            counts[i] = counts[i] + extra
            spare = spare - extra
    return np.array([most] + counts)


def uneven(stream_key, number_of, total, limit, skew):
    if number_of == 2:
        one = jax.random.randint(stream_key, (), max(1, total - limit), min(limit, total - 1) + 1)
        return jnp.stack([one, total - one])
    sizes = jnp.asarray(profile(number_of, total, limit, skew), jnp.int32)
    couples = (number_of - 1) // 2
    giver, sink = sizes[1:1 + 2 * couples:2], sizes[2:2 + 2 * couples:2]
    room = jnp.minimum(giver - 1, limit - sink)
    shifted = jax.random.randint(jax.random.fold_in(stream_key, 1), (couples,), 0, 1 << 20) % (room + 1)
    sizes = sizes.at[1:1 + 2 * couples:2].set(giver - shifted).at[2:2 + 2 * couples:2].set(sink + shifted)
    return sizes[jax.random.permutation(jax.random.fold_in(stream_key, 2), number_of)]


def normal_values(rng, extent, spread, limit, pieces=(), kind=jnp.bfloat16):
    array = spread * jax.random.normal(rng, extent, jnp.float32)
    if pieces:
        array = array * steps_of(rng, extent, pieces, -0.22, 0.18)
    return jnp.clip(array, -limit, limit).astype(kind)


def setup_inputs(seed: int = 0) -> dict:
    seeds = jax.random.split(jax.random.key(seed), 7)
    return {
        "normed": normal_values(seeds[0], (BATCHES, SEQ, D), 1.0, 6.0, ((0, 8), (1, 16))),
        "queries": draw_queries(jax.random.fold_in(seeds[6], 71), 0),
        "cotangent": normal_values(seeds[2], (BATCHES, SEQ, QW), 1.0, 6.0, ((0, 8), (1, 16))),
        "lengths": jax.vmap(lambda own: uneven(own, NDOC, SEQ, LMAX, 2))(jax.random.split(seeds[3], BATCHES)).reshape((BATCHES, NDOC)).astype(jnp.int32),
        "balanced_slot": draw_balanced_slot(jax.random.fold_in(seeds[6], 71), 0),
        "kv_weight": normal_values(seeds[5], (D, 2 * KVW), D ** -0.5, 0.09375),
    }


def visible_mask(lengths_row, row_pos, key_pos):
    doc_ends = jnp.cumsum(lengths_row).astype(jnp.int32)
    row_doc = jnp.sum((row_pos[:, None] >= doc_ends[None, :]).astype(jnp.int32), axis=1)
    key_doc = jnp.sum((key_pos[:, None] >= doc_ends[None, :]).astype(jnp.int32), axis=1)
    return (row_doc[:, None] == key_doc[None, :]) & (key_pos[None, :] <= row_pos[:, None])


def head_pass(query_h, key_h, value_h, grad_h, visible):
    scale = HD ** -0.5
    query_f = query_h.astype(jnp.float32)
    key_f = key_h.astype(jnp.float32)
    value_f = value_h.astype(jnp.float32)
    grad_f = grad_h.astype(jnp.float32)
    scores = jnp.einsum('grd,sd->grs', query_f, key_f) * scale
    scores = jnp.where(visible[None], scores, jnp.float32(-1e30))
    peak = jnp.max(scores, axis=-1, keepdims=True)
    expo = jnp.exp(scores - peak)
    prob_f32 = expo / jnp.sum(expo, axis=-1, keepdims=True)
    prob_b16 = prob_f32.astype(jnp.bfloat16).astype(jnp.float32)
    head_out = jnp.einsum('grs,sd->grd', prob_b16, value_f)
    grad_probs = jnp.einsum('grd,sd->grs', grad_f, value_f)
    row_delta = jnp.sum(grad_f * head_out, axis=-1)
    grad_scores = (prob_f32 * (grad_probs - row_delta[..., None]) * scale).astype(jnp.bfloat16).astype(jnp.float32)
    grad_query = jnp.einsum('grs,sd->grd', grad_scores, key_f)
    grad_key = jnp.einsum('grs,grd->sd', grad_scores, query_f)
    grad_value = jnp.einsum('grs,grd->sd', prob_b16, grad_f)
    return head_out, grad_query, grad_key, grad_value


def reference(normed, queries, cotangent, lengths, balanced_slot, kv_weight):
    def one_batch(pack):
        inputs, query_rows, grad_bal, lengths_row, slots = pack
        kv_rows = jnp.dot(inputs, kv_weight, preferred_element_type=jnp.float32).astype(jnp.bfloat16)
        positions = jnp.arange(SEQ, dtype=jnp.int32)
        grad_even = grad_bal[slots.astype(jnp.int32)]
        visible = visible_mask(lengths_row, positions, positions)
        query4 = query_rows.reshape(SEQ, KVH, GROUP, HD).transpose(1, 2, 0, 3)
        grad4 = grad_even.reshape(SEQ, KVH, GROUP, HD).transpose(1, 2, 0, 3)
        key3 = kv_rows[:, :KVW].reshape(SEQ, KVH, HD).transpose(1, 0, 2)
        value3 = kv_rows[:, KVW:].reshape(SEQ, KVH, HD).transpose(1, 0, 2)
        head_out, grad_query, grad_key, grad_value = lax.map(
            lambda item: head_pass(item[0], item[1], item[2], item[3], visible), (query4, key3, value3, grad4))
        attn_even = head_out.transpose(2, 0, 1, 3).reshape(SEQ, QW).astype(jnp.bfloat16)
        attn_bal = jnp.zeros((SEQ, QW), jnp.bfloat16).at[slots.astype(jnp.int32)].set(attn_even)
        query_grad = grad_query.transpose(2, 0, 1, 3).reshape(SEQ, QW).astype(jnp.bfloat16)
        kv_grad = jnp.concatenate([grad_key.transpose(1, 0, 2).reshape(SEQ, KVW),
                                   grad_value.transpose(1, 0, 2).reshape(SEQ, KVW)], axis=1).astype(jnp.bfloat16)
        input_grad = jnp.dot(kv_grad, kv_weight.T, preferred_element_type=jnp.float32).astype(jnp.bfloat16)
        weight_part = jnp.dot(inputs.T, kv_grad, preferred_element_type=jnp.float32)
        return attn_bal, query_grad, input_grad, weight_part

    attn_out, q_grad, input_grad, weight_parts = lax.map(one_batch, (normed, queries, cotangent, lengths, balanced_slot))
    weight_grad = jnp.sum(weight_parts, axis=0)
    return attn_out, q_grad, input_grad, weight_grad
```

```python
import math

import jax
import jax.numpy as jnp
from jax import lax
from jax.experimental import pallas as pl
from jax.experimental.pallas import tpu as pltpu
from jax.sharding import Mesh
from jax.sharding import PartitionSpec as P

HD = 128
BLOCK = 128
TILE = 256
SEQ = 2048
DOCS = 8
MAXTILES = 5
SCALE = HD ** (-0.5)
CTX = ("z", "y")
NN = (((1,), (0,)), ((), ()))
NT = (((1,), (1,)), ((), ()))


def dot32(a, b, dims=NN):
    return lax.dot_general(a, b, dims, preferred_element_type=jnp.float32)


def attend_kernel(len_ref, a_ref, kv_ref, o_ref, dkv_ref, kt_ref, vt_ref, acc_ref):
    tiles = SEQ // TILE
    for t in range(tiles):
        kv = kv_ref[2 * t : 2 * t + 2].reshape(TILE, 2 * HD)
        kt_ref[t] = kv[:, :HD].T
        vt_ref[t] = kv[:, HD:].T
    acc_ref[...] = jnp.zeros_like(acc_ref)

    def tile_step(i, carry):
        base = i * TILE
        ends = []
        total = jnp.int32(0)
        for d in range(DOCS):
            total = total + len_ref[0, d]
            ends.append(total)
        first = jnp.int32(0)
        for end in ends:
            first = jnp.where(end <= base, end, first)
        first_tile = first // TILE
        count = i - first_tile + 1
        q_pos = base + lax.broadcasted_iota(jnp.int32, (1, TILE), 1)
        q_start = jnp.zeros((1, TILE), jnp.int32)
        for end in ends:
            q_start = jnp.where(end <= q_pos, end, q_start)
        down = lax.broadcasted_iota(jnp.int32, (TILE, TILE), 0)

        def work(n):
            q = a_ref[pl.ds(2 * i, 2), 0:BLOCK, :].reshape(TILE, HD)
            places = a_ref[pl.ds(2 * i, 2), 2 * BLOCK : 2 * BLOCK + 16, :].astype(jnp.float32)
            place = jnp.concatenate([places[0, 0:1], places[1, 0:1]], axis=1)
            onehot = (down == place.astype(jnp.int32)).astype(jnp.bfloat16)
            g_bal = a_ref[:, pl.ds(pl.multiple_of(BLOCK + 16 * i, 16), 16), :].reshape(TILE, HD)
            gt32 = dot32(g_bal.T, onehot)
            gt = gt32.astype(jnp.bfloat16)
            g = gt.T
            scores = []
            for j in range(n):
                tile = first_tile + j
                key = kv_ref[pl.ds(2 * tile, 2), :, 0:HD].reshape(TILE, HD)
                raw = dot32(key, q, NT)
                k_pos = tile * TILE + down
                seen = k_pos >= q_start
                if j == n - 1:
                    seen = seen & (k_pos <= q_pos)
                scores.append(jnp.where(seen, raw, jnp.float32(-1e30)))
            peak = scores[0]
            for s in scores[1:]:
                peak = jnp.maximum(peak, s)
            peak = jnp.max(peak, axis=0, keepdims=True)
            expo = [jnp.exp2((s - peak) * (SCALE * math.log2(math.e))) for s in scores]
            norm = expo[0]
            for e in expo[1:]:
                norm = norm + e
            inv = 1.0 / jnp.sum(norm, axis=0, keepdims=True)
            prob = [e * inv for e in expo]
            prob16 = [p.astype(jnp.bfloat16) for p in prob]
            out_t = jnp.zeros((HD, TILE), jnp.float32)
            for j in range(n):
                out_t = out_t + dot32(vt_ref[first_tile + j], prob16[j])
            delta = jnp.sum(gt32 * out_t, axis=0, keepdims=True)
            out_bal = dot32(onehot, out_t.astype(jnp.bfloat16), NT).astype(jnp.bfloat16)
            o_ref[:, pl.ds(pl.multiple_of(16 * i, 16), 16), :] = out_bal.reshape(16, 16, HD)
            dq_t = jnp.zeros((HD, TILE), jnp.float32)
            for j in range(n):
                tile = first_tile + j
                value = kv_ref[pl.ds(2 * tile, 2), :, HD : 2 * HD].reshape(TILE, HD)
                grad_prob = dot32(value, g, NT)
                grad_score = (prob[j] * (grad_prob - delta) * SCALE).astype(jnp.bfloat16)
                dq_t = dq_t + dot32(kt_ref[tile], grad_score)
                acc_ref[tile, :, 0:HD] += dot32(grad_score, q)
                acc_ref[tile, :, HD : 2 * HD] += dot32(prob16[j], g)
            o_ref[pl.ds(2 * i, 2), BLOCK : 2 * BLOCK, :] = (
                dq_t.astype(jnp.bfloat16).T.reshape(2, BLOCK, HD)
            )

        for n in range(1, MAXTILES + 1):
            pl.when(count == n)(lambda n=n: work(n))
        return carry

    lax.fori_loop(0, tiles, tile_step, 0)
    for t in range(tiles):
        dkv_ref[2 * t : 2 * t + 2] = acc_ref[t].astype(jnp.bfloat16).reshape(2, BLOCK, 2 * HD)


def attend(lengths, rows, kv):
    ways = rows.shape[0]
    tiles = SEQ // TILE
    vmem = pl.BlockSpec(memory_space=pltpu.VMEM)
    return pl.pallas_call(
        attend_kernel,
        out_shape=(
            jax.ShapeDtypeStruct((ways, 2 * BLOCK, HD), jnp.bfloat16),
            jax.ShapeDtypeStruct((ways, BLOCK, 2 * HD), jnp.bfloat16),
        ),
        in_specs=[pl.BlockSpec(memory_space=pltpu.SMEM), vmem, vmem],
        out_specs=(vmem, vmem),
        scratch_shapes=[
            pltpu.VMEM((tiles, HD, TILE), jnp.bfloat16),
            pltpu.VMEM((tiles, HD, TILE), jnp.bfloat16),
            pltpu.VMEM((tiles, TILE, 2 * HD), jnp.float32),
        ],
        compiler_params=pltpu.CompilerParams(vmem_limit_bytes=40 * 1024 * 1024),
        cost_estimate=pl.CostEstimate(
            flops=6 * 2 * SEQ * 640 * HD, bytes_accessed=6 * 1024 * 1024, transcendentals=SEQ * 640
        ),
        name="attend",
    )(lengths, rows, kv)


def ring_all(block, axis):
    def shift(v, k):
        return lax.ppermute(v, axis, [(s, (s + k) % 4) for s in range(4)])

    here = lax.axis_index(axis)
    left = shift(block, 1)
    right = shift(block, -1)
    half = block.shape[0] // 2
    across = jnp.concatenate([shift(left[:half], 1), shift(right[half:], -1)], axis=0)
    ordered = jnp.stack([block, left, across, right])
    return jnp.stack([lax.dynamic_index_in_dim(ordered, (here - s) % 4, 0, False) for s in range(4)])


def per_device(normed, queries, cotangent, lengths, balanced_slot, kv_weight):
    inputs = normed[0]
    heads = 16
    slots = balanced_slot[0]
    place = (slots // BLOCK * 16 + slots % 16).astype(jnp.bfloat16)
    rows = jnp.concatenate(
        [
            queries[0].reshape(BLOCK, heads, HD).transpose(1, 0, 2),
            cotangent[0].reshape(BLOCK, heads, HD).transpose(1, 0, 2),
            jnp.broadcast_to(place, (heads, 16, BLOCK)),
        ],
        axis=1,
    )
    rows = lax.all_to_all(rows, CTX, 0, 0, tiled=True)
    kv_rows = jnp.dot(inputs, kv_weight, preferred_element_type=jnp.float32).astype(jnp.bfloat16)
    kv4 = kv_rows.reshape(BLOCK, 2, 4, HD).transpose(2, 0, 1, 3).reshape(4, 1, BLOCK, 2 * HD)
    kv_send = jnp.broadcast_to(kv4, (4, 4, BLOCK, 2 * HD)).reshape(heads, BLOCK, 2 * HD)
    kv = lax.all_to_all(kv_send, CTX, 0, 0, tiled=True)

    out, dkv = attend(lengths, rows, kv)

    dkv = dkv.reshape(4, 4, BLOCK, 2 * HD).transpose(1, 0, 2, 3)
    dkv = lax.all_to_all(dkv, "y", 0, 0, tiled=True)
    dkv = jnp.sum(dkv.astype(jnp.float32), axis=0).astype(jnp.bfloat16)

    back = lax.all_to_all(out, CTX, 0, 0, tiled=True)
    attn_out = back[:, :BLOCK].transpose(1, 0, 2).reshape(BLOCK, heads * HD)
    q_grad = back[:, BLOCK:].transpose(1, 0, 2).reshape(BLOCK, heads * HD)

    own = lax.all_to_all(dkv, "z", 0, 0, tiled=True)
    kv_grad = own.reshape(4, BLOCK, 2, HD).transpose(1, 2, 0, 3).reshape(BLOCK, 8 * HD)
    input_grad = lax.dot_general(
        kv_grad, kv_weight, NT, preferred_element_type=jnp.float32
    ).astype(jnp.bfloat16)

    normed_z = ring_all(inputs, "z").reshape(4 * BLOCK, -1)
    part = lax.dot_general(
        normed_z, dkv.reshape(4 * BLOCK, 2 * HD), (((0,), (0,)), ((), ())),
        preferred_element_type=jnp.float32,
    )
    part = part.reshape(4, 2, 4, 4, 32, 2 * HD)
    core = lax.axis_index("core")
    keep = lax.dynamic_index_in_dim(part, core, 1, False)
    give = lax.dynamic_index_in_dim(part, 1 - core, 1, False).astype(jnp.bfloat16)
    take = lax.ppermute(give, "core", [(0, 1), (1, 0)])
    both = (keep + take.astype(jnp.float32)).astype(jnp.bfloat16).reshape(64, 32, 2 * HD)
    got = lax.all_to_all(both, ("x", "z", "y"), 0, 0, tiled=True)
    got = got.reshape(4, 4, 4, 32, 2, HD).astype(jnp.float32).sum(axis=(0, 2))
    weight_grad = got.transpose(1, 2, 0, 3).reshape(32, 8 * HD)
    return (attn_out[None], q_grad[None], input_grad[None], weight_grad)


def solution(mesh):
    fine = Mesh(mesh.devices.reshape(4, 2, 4, 4), ("x", "core", "z", "y"))
    dp = ("x", "core")
    placed = (
        P(dp, CTX, None),
        P(dp, CTX, None),
        P(dp, CTX, None),
        P(dp, None),
        P(dp, CTX),
        P(),
    )
    return jax.shard_map(
        per_device,
        mesh=fine,
        in_specs=placed,
        out_specs=(
            P(dp, CTX, None),
            P(dp, CTX, None),
            P(dp, CTX, None),
            P(dp + CTX, None),
        ),
        check_vma=False,
    )
```

```python
import math

import jax
import jax.numpy as jnp
from jax import lax
from jax.experimental import pallas as pl
from jax.experimental.pallas import tpu as pltpu
from jax.sharding import Mesh
from jax.sharding import PartitionSpec as P

HD = 128
BLOCK = 128
TILE = 256
SEQ = 2048
DOCS = 8
MAXTILES = 5
SCALE = HD ** (-0.5)
HEADS = 16
CTX = ("z", "y")
VMEM = pl.BlockSpec(memory_space=pltpu.VMEM)
SMEM = pl.BlockSpec(memory_space=pltpu.SMEM)
NN = (((1,), (0,)), ((), ()))
NT = (((1,), (1,)), ((), ()))


def dot32(a, b, dims=NN):
    return lax.dot_general(a, b, dims, preferred_element_type=jnp.float32)


def pack_kernel(q_ref, g_ref, slot_ref, o_ref):
    slots = slot_ref[0:1, :]
    place = ((slots >> 7) * 16 + (slots & 15)).astype(jnp.float32)
    place = jnp.broadcast_to(place, (16, BLOCK)).astype(jnp.bfloat16)
    for h in range(HEADS):
        o_ref[h, 0:BLOCK] = q_ref[:, h * HD : (h + 1) * HD]
        o_ref[h, BLOCK : 2 * BLOCK] = g_ref[:, h * HD : (h + 1) * HD]
        o_ref[h, 2 * BLOCK :] = place


def pack(queries, cotangent, slots):
    return pl.pallas_call(
        pack_kernel,
        out_shape=jax.ShapeDtypeStruct((HEADS, 2 * BLOCK + 16, HD), jnp.bfloat16),
        in_specs=[VMEM, VMEM, VMEM],
        out_specs=VMEM,
        cost_estimate=pl.CostEstimate(flops=0, bytes_accessed=2 * 1024 * 1024, transcendentals=0),
        name="pack",
    )(queries, cotangent, slots)


def project_kernel(at_ref, x_ref, w_ref, o0_ref, o1_ref, o2_ref, o3_ref, acc_ref, head_ref):
    step = pl.program_id(0)

    @pl.when(step == 0)
    def _():
        acc_ref[...] = jnp.zeros_like(acc_ref)

    acc_ref[...] += dot32(x_ref[...], w_ref[...])

    @pl.when(step == pl.num_programs(0) - 1)
    def _():
        for h in range(4):
            head_ref[h, :, 0:HD] = acc_ref[:, h * HD : (h + 1) * HD].astype(jnp.bfloat16)
            head_ref[h, :, HD:] = acc_ref[:, (h + 4) * HD : (h + 5) * HD].astype(jnp.bfloat16)
        for k, o_ref in enumerate((o0_ref, o1_ref, o2_ref, o3_ref)):
            o_ref[...] = head_ref[(at_ref[0] + k) & 3]


def project(place, inputs, weight):
    width = inputs.shape[1]
    chunk = 512
    piece = jax.ShapeDtypeStruct((BLOCK, 2 * HD), jnp.bfloat16)
    whole = pl.BlockSpec((BLOCK, 2 * HD), lambda i: (0, 0))
    return pl.pallas_call(
        project_kernel,
        grid=(width // chunk,),
        out_shape=(piece,) * 4,
        in_specs=[
            SMEM,
            pl.BlockSpec((BLOCK, chunk), lambda i: (0, i)),
            pl.BlockSpec((chunk, 8 * HD), lambda i: (i, 0)),
        ],
        out_specs=(whole,) * 4,
        scratch_shapes=[
            pltpu.VMEM((BLOCK, 8 * HD), jnp.float32),
            pltpu.VMEM((4, BLOCK, 2 * HD), jnp.bfloat16),
        ],
        cost_estimate=pl.CostEstimate(
            flops=2 * BLOCK * width * 8 * HD, bytes_accessed=10 * 1024 * 1024, transcendentals=0
        ),
        name="project",
    )(place, inputs, weight)


def attend_kernel(
    len_ref, at_ref, a_ref, kv0_ref, kv1_ref, kv2_ref, kv3_ref,
    o_ref, d0_ref, d1_ref, d2_ref, d3_ref, kv_ref, kt_ref, vt_ref, acc_ref,
):
    tiles = SEQ // TILE
    z = at_ref[0]
    y = at_ref[1]
    for a, piece in enumerate((kv0_ref, kv1_ref, kv2_ref, kv3_ref)):
        for k in range(4):
            kv_ref[((z + 4 - k) & 3) * 4 + ((y + 4 - a) & 3)] = piece[k]
    for t in range(tiles):
        kv = kv_ref[2 * t : 2 * t + 2].reshape(TILE, 2 * HD)
        kt_ref[t] = kv[:, :HD].T
        vt_ref[t] = kv[:, HD:].T
    acc_ref[...] = jnp.zeros_like(acc_ref)

    def tile_step(i, carry):
        base = i * TILE
        ends = []
        total = jnp.int32(0)
        for d in range(DOCS):
            total = total + len_ref[0, d]
            ends.append(total)
        first = jnp.int32(0)
        for end in ends:
            first = jnp.where(end <= base, end, first)
        first_tile = first // TILE
        count = i - first_tile + 1
        q_pos = base + lax.broadcasted_iota(jnp.int32, (1, TILE), 1)
        q_start = jnp.zeros((1, TILE), jnp.int32)
        for end in ends:
            q_start = jnp.where(end <= q_pos, end, q_start)
        down = lax.broadcasted_iota(jnp.int32, (TILE, TILE), 0)

        def work(n):
            q = a_ref[pl.ds(2 * i, 2), 0:BLOCK, :].reshape(TILE, HD)
            places = a_ref[pl.ds(2 * i, 2), 2 * BLOCK : 2 * BLOCK + 16, :].astype(jnp.float32)
            place = jnp.concatenate([places[0, 0:1], places[1, 0:1]], axis=1)
            onehot = (down == place.astype(jnp.int32)).astype(jnp.bfloat16)
            g_bal = a_ref[:, pl.ds(pl.multiple_of(BLOCK + 16 * i, 16), 16), :].reshape(TILE, HD)
            gt32 = dot32(g_bal.T, onehot)
            gt = gt32.astype(jnp.bfloat16)
            g = gt.T
            scores = []
            for j in range(n):
                tile = first_tile + j
                key = kv_ref[pl.ds(2 * tile, 2), :, 0:HD].reshape(TILE, HD)
                raw = dot32(key, q, NT)
                k_pos = tile * TILE + down
                seen = k_pos >= q_start
                if j == n - 1:
                    seen = seen & (k_pos <= q_pos)
                scores.append(jnp.where(seen, raw, jnp.float32(-1e30)))
            peak = scores[0]
            for s in scores[1:]:
                peak = jnp.maximum(peak, s)
            peak = jnp.max(peak, axis=0, keepdims=True)
            expo = [jnp.exp2((s - peak) * (SCALE * math.log2(math.e))) for s in scores]
            norm = expo[0]
            for e in expo[1:]:
                norm = norm + e
            inv = 1.0 / jnp.sum(norm, axis=0, keepdims=True)
            prob = [e * inv for e in expo]
            prob16 = [p.astype(jnp.bfloat16) for p in prob]
            out_t = jnp.zeros((HD, TILE), jnp.float32)
            for j in range(n):
                out_t = out_t + dot32(vt_ref[first_tile + j], prob16[j])
            delta = jnp.sum(gt32 * out_t, axis=0, keepdims=True)
            out_bal = dot32(onehot, out_t.astype(jnp.bfloat16), NT).astype(jnp.bfloat16)
            o_ref[:, pl.ds(pl.multiple_of(16 * i, 16), 16), :] = out_bal.reshape(16, 16, HD)
            dq_t = jnp.zeros((HD, TILE), jnp.float32)
            for j in range(n):
                tile = first_tile + j
                value = kv_ref[pl.ds(2 * tile, 2), :, HD : 2 * HD].reshape(TILE, HD)
                grad_prob = dot32(value, g, NT)
                grad_score = (prob[j] * (grad_prob - delta) * SCALE).astype(jnp.bfloat16)
                dq_t = dq_t + dot32(kt_ref[tile], grad_score)
                acc_ref[pl.ds(2 * tile, 2), :, 0:HD] += dot32(grad_score, q).reshape(2, BLOCK, HD)
                acc_ref[pl.ds(2 * tile, 2), :, HD : 2 * HD] += dot32(prob16[j], g).reshape(
                    2, BLOCK, HD
                )
            o_ref[pl.ds(2 * i, 2), BLOCK : 2 * BLOCK, :] = (
                dq_t.astype(jnp.bfloat16).T.reshape(2, BLOCK, HD)
            )

        for n in range(1, MAXTILES + 1):
            pl.when(count == n)(lambda n=n: work(n))
        return carry

    lax.fori_loop(0, tiles, tile_step, 0)
    for a, piece in enumerate((d0_ref, d1_ref, d2_ref, d3_ref)):
        for k in range(4):
            piece[k] = acc_ref[((z + 4 - k) & 3) * 4 + ((y + a) & 3)].astype(piece.dtype)


def attend(lengths, place, rows, kv):
    ways = rows.shape[0]
    tiles = SEQ // TILE
    piece = (4, BLOCK, 2 * HD)
    return pl.pallas_call(
        attend_kernel,
        out_shape=(
            jax.ShapeDtypeStruct((ways, 2 * BLOCK, HD), jnp.bfloat16),
            jax.ShapeDtypeStruct(piece, jnp.float32),
            jax.ShapeDtypeStruct(piece, jnp.bfloat16),
            jax.ShapeDtypeStruct(piece, jnp.bfloat16),
            jax.ShapeDtypeStruct(piece, jnp.bfloat16),
        ),
        in_specs=[SMEM, SMEM] + [VMEM] * 5,
        out_specs=(VMEM,) * 5,
        scratch_shapes=[
            pltpu.VMEM((ways, BLOCK, 2 * HD), jnp.bfloat16),
            pltpu.VMEM((tiles, HD, TILE), jnp.bfloat16),
            pltpu.VMEM((tiles, HD, TILE), jnp.bfloat16),
            pltpu.VMEM((ways, BLOCK, 2 * HD), jnp.float32),
        ],
        compiler_params=pltpu.CompilerParams(vmem_limit_bytes=40 * 1024 * 1024),
        cost_estimate=pl.CostEstimate(
            flops=12 * 2 * SEQ * 640 * HD, bytes_accessed=6 * 1024 * 1024, transcendentals=SEQ * 640
        ),
        name="attend",
    )(lengths, place, rows, *kv)


def weigh_kernel(
    at_ref, m_ref, t_ref, n0_ref, n1_ref, n2a_ref, n2b_ref, n3_ref,
    w0_ref, w1_ref, w2_ref, w3_ref, d_ref,
):
    for k in range(4):
        d_ref[k, :, 0:BLOCK] = m_ref[k].T
        d_ref[k, :, BLOCK:] = t_ref[k].T
    for a, o_ref in enumerate((w0_ref, w1_ref, w2_ref, w3_ref)):
        chunk = (at_ref[2] + a) & 3
        across = jnp.where(chunk < 2, n2a_ref[chunk & 1], n2b_ref[chunk & 1])
        total = dot32(d_ref[0], n0_ref[chunk])
        total = total + dot32(d_ref[1], n1_ref[chunk])
        total = total + dot32(d_ref[2], across)
        total = total + dot32(d_ref[3], n3_ref[chunk])
        o_ref[...] = total.astype(o_ref.dtype)


def weigh(place, mine, theirs, blocks):
    piece = (2 * HD, 512)
    return pl.pallas_call(
        weigh_kernel,
        out_shape=(jax.ShapeDtypeStruct(piece, jnp.float32),)
        + (jax.ShapeDtypeStruct(piece, jnp.bfloat16),) * 3,
        in_specs=[SMEM] + [VMEM] * 7,
        out_specs=(VMEM,) * 4,
        scratch_shapes=[pltpu.VMEM((4, 2 * HD, 2 * BLOCK), jnp.bfloat16)],
        compiler_params=pltpu.CompilerParams(vmem_limit_bytes=32 * 1024 * 1024),
        cost_estimate=pl.CostEstimate(
            flops=2 * 2 * HD * 2048 * 1024, bytes_accessed=6 * 1024 * 1024, transcendentals=0
        ),
        name="weigh",
    )(place, mine, theirs, *blocks)


def fold_kernel(w0_ref, w1_ref, w2_ref, w3_ref, o_ref):
    total = w0_ref[...] + w1_ref[...].astype(jnp.float32)
    total = total + w2_ref[...].astype(jnp.float32) + w3_ref[...].astype(jnp.float32)
    o_ref[...] = total.T.astype(jnp.bfloat16).reshape(o_ref.shape)


def fold(pieces):
    return pl.pallas_call(
        fold_kernel,
        out_shape=jax.ShapeDtypeStruct((16, 32, 2 * HD), jnp.bfloat16),
        in_specs=[VMEM] * 4,
        out_specs=VMEM,
        name="fold",
    )(*pieces)


def close_kernel(p_ref, o_ref):
    for h in range(4):
        total = p_ref[4 * h].astype(jnp.float32)
        for s in range(1, 4):
            total = total + p_ref[4 * h + s].astype(jnp.float32)
        o_ref[:, h * HD : (h + 1) * HD] = total[:, :HD]
        o_ref[:, (h + 4) * HD : (h + 5) * HD] = total[:, HD:]


def close(parts):
    return pl.pallas_call(
        close_kernel,
        out_shape=jax.ShapeDtypeStruct((32, 8 * HD), jnp.float32),
        in_specs=[VMEM],
        out_specs=VMEM,
        name="close",
    )(parts)


def shift(v, axis, k):
    return lax.ppermute(v, axis, [(s, (s + k) % 4) for s in range(4)])


def swap(v):
    return lax.ppermute(v, "core", [(0, 1), (1, 0)])


def per_device(normed, queries, cotangent, lengths, balanced_slot, kv_weight):
    inputs = normed[0]
    x, core, z, y = (lax.axis_index(name) for name in ("x", "core", "z", "y"))
    place = jnp.stack([z, y, x]).astype(jnp.int32)

    mine = project(place, inputs, kv_weight)
    kv = [mine[0]] + [shift(mine[k], "z", k) for k in (1, 2, 3)]
    rows = lax.all_to_all(
        pack(queries[0], cotangent[0], balanced_slot), CTX, 0, 0, tiled=True
    )
    kv = jnp.stack(kv)
    kv = [kv] + [shift(kv, "y", k) for k in (1, 2, 3)]

    halves = inputs.reshape(BLOCK, 4, 2, 512)
    keep = lax.dynamic_index_in_dim(halves, core, 2, False).transpose(1, 0, 2)
    give = lax.dynamic_index_in_dim(halves, 1 - core, 2, False).transpose(1, 0, 2)
    tokens = jnp.concatenate([keep, swap(give)], axis=1)
    rows, kv, tokens = lax.optimization_barrier((rows, kv, tokens))
    left = shift(tokens, "z", 1)
    right = shift(tokens, "z", -1)

    out, *dkv = attend(lengths, place, rows, kv)

    dkv = [dkv[0]] + [shift(dkv[k], "y", k).astype(jnp.float32) for k in (1, 2, 3)]
    dkv = (dkv[0] + dkv[1] + dkv[2] + dkv[3]).astype(jnp.bfloat16)

    back = lax.all_to_all(out, CTX, 0, 0, tiled=True)
    attn_out = back[:, :BLOCK].transpose(1, 0, 2).reshape(BLOCK, HEADS * HD)
    q_grad = back[:, BLOCK:].transpose(1, 0, 2).reshape(BLOCK, HEADS * HD)

    left, right, dkv = lax.optimization_barrier((left, right, dkv))
    across_a = shift(left[:2], "z", 1)
    across_b = shift(right[2:], "z", -1)
    pieces = weigh(place, dkv, swap(dkv), (tokens, left, across_a, across_b, right))
    pieces = [pieces[0]] + [shift(pieces[k], "x", k) for k in (1, 2, 3)]
    parts = lax.all_to_all(fold(pieces), CTX, 0, 0, tiled=True)
    weight_grad = close(parts)

    own = jnp.stack([dkv[0]] + [shift(dkv[k], "z", -k) for k in (1, 2, 3)])
    own = jnp.stack([lax.dynamic_index_in_dim(own, (h - z) % 4, 0, False) for h in range(4)])
    kv_grad = own.reshape(4, BLOCK, 2, HD).transpose(1, 2, 0, 3).reshape(BLOCK, 8 * HD)
    input_grad = lax.dot_general(
        kv_grad, kv_weight, NT, preferred_element_type=jnp.float32
    ).astype(jnp.bfloat16)
    return (attn_out[None], q_grad[None], input_grad[None], weight_grad)


def solution(mesh):
    fine = Mesh(mesh.devices.reshape(4, 2, 4, 4), ("x", "core", "z", "y"))
    dp = ("x", "core")
    placed = (
        P(dp, CTX, None),
        P(dp, CTX, None),
        P(dp, CTX, None),
        P(dp, None),
        P(dp, CTX),
        P(),
    )
    return jax.shard_map(
        per_device,
        mesh=fine,
        in_specs=placed,
        out_specs=(
            P(dp, CTX, None),
            P(dp, CTX, None),
            P(dp, CTX, None),
            P(dp + CTX, None),
        ),
        check_vma=False,
    )
```

```python
import math

import jax
import jax.numpy as jnp
from jax import lax
from jax.experimental import pallas as pl
from jax.experimental.pallas import tpu as pltpu
from jax.sharding import Mesh
from jax.sharding import PartitionSpec as P

HD = 128
BLOCK = 128
TILE = 256
SEQ = 2048
DOCS = 8
MAXTILES = 5
SCALE = HD ** (-0.5)
HEADS = 16
CTX = ("z", "y")
VMEM = pl.BlockSpec(memory_space=pltpu.VMEM)
SMEM = pl.BlockSpec(memory_space=pltpu.SMEM)
HBM = pl.BlockSpec(memory_space=pltpu.HBM)
ANY = pl.BlockSpec(memory_space=pl.ANY)
NN = (((1,), (0,)), ((), ()))
NT = (((1,), (1,)), ((), ()))


def grant(mib):
    return pltpu.CompilerParams(vmem_limit_bytes=mib * 1024 * 1024)


def dot32(a, b, dims=NN):
    return lax.dot_general(a, b, dims, preferred_element_type=jnp.float32)


def project_kernel(
    at_ref, x_hbm, w_hbm, after_ref, o0_hbm, o1_hbm, o2_hbm, o3_hbm, keep_hbm, give_hbm,
    x_ref, w_ref, head_ref, x_sem, w_sem, out_sem, col_sem,
):
    steps = w_ref.shape[0]
    width = w_ref.shape[1]
    whole = pltpu.make_async_copy(x_hbm, x_ref, x_sem)
    weights = [
        pltpu.make_async_copy(w_hbm.at[pl.ds(s * width, width)], w_ref.at[s], w_sem.at[s])
        for s in range(steps)
    ]
    whole.start()
    for copy in weights:
        copy.start()
    whole.wait()
    columns = []
    for c in range(4):
        for other, o_hbm in enumerate((keep_hbm, give_hbm)):
            half = at_ref[3] if other == 0 else 1 - at_ref[3]
            start = pl.multiple_of(c * 1024 + half * 512, 512)
            columns.append(
                pltpu.make_async_copy(
                    x_ref.at[:, pl.ds(start, 512)], o_hbm.at[c], col_sem.at[2 * c + other]
                )
            )
    total = jnp.zeros((BLOCK, 8 * HD), jnp.float32)
    for s in range(steps):
        weights[s].wait()
        total = total + dot32(x_ref[:, s * width : (s + 1) * width], w_ref[s])
    for h in range(4):
        head_ref[h, :, 0:HD] = total[:, h * HD : (h + 1) * HD].astype(jnp.bfloat16)
        head_ref[h, :, HD:] = total[:, (h + 4) * HD : (h + 5) * HD].astype(jnp.bfloat16)
    out = [
        pltpu.make_async_copy(head_ref.at[(at_ref[0] + k) & 3], o_hbm, out_sem.at[k])
        for k, o_hbm in enumerate((o0_hbm, o1_hbm, o2_hbm, o3_hbm))
    ]
    for copy in out + columns:
        copy.start()
    for copy in out + columns:
        copy.wait()


def project(place, inputs, weight, after):
    width = inputs.shape[1]
    chunk = 512
    piece = jax.ShapeDtypeStruct((BLOCK, 2 * HD), jnp.bfloat16)
    half = jax.ShapeDtypeStruct((4, BLOCK, 512), jnp.bfloat16)
    return pl.pallas_call(
        project_kernel,
        out_shape=(piece,) * 4 + (half, half),
        in_specs=[SMEM, HBM, HBM, ANY],
        out_specs=(HBM,) * 6,
        scratch_shapes=[
            pltpu.VMEM(inputs.shape, jnp.bfloat16),
            pltpu.VMEM((width // chunk, chunk, 8 * HD), jnp.bfloat16),
            pltpu.VMEM((4, BLOCK, 2 * HD), jnp.bfloat16),
            pltpu.SemaphoreType.DMA,
            pltpu.SemaphoreType.DMA((width // chunk,)),
            pltpu.SemaphoreType.DMA((4,)),
            pltpu.SemaphoreType.DMA((8,)),
        ],
        compiler_params=grant(58),
        cost_estimate=pl.CostEstimate(
            flops=2 * BLOCK * width * 8 * HD, bytes_accessed=14 * 1024 * 1024, transcendentals=0
        ),
        name="project",
    )(place, inputs, weight, after)


def pack_kernel(slot_ref, q_ref, g_ref, rows_ref):
    slots = slot_ref[0:1, :]
    place = ((slots >> 7) * 16 + (slots & 15)).astype(jnp.float32)
    place = jnp.broadcast_to(place, (16, BLOCK)).astype(jnp.bfloat16)
    for h in range(HEADS):
        rows_ref[h, 0:BLOCK] = q_ref[:, h * HD : (h + 1) * HD]
        rows_ref[h, BLOCK : 2 * BLOCK] = g_ref[:, h * HD : (h + 1) * HD]
        rows_ref[h, 2 * BLOCK :] = place


def pack(slots, queries, cotangent):
    return pl.pallas_call(
        pack_kernel,
        out_shape=jax.ShapeDtypeStruct((HEADS, 2 * BLOCK + 16, HD), jnp.bfloat16),
        in_specs=[VMEM, VMEM, VMEM],
        out_specs=VMEM,
        compiler_params=grant(58),
        cost_estimate=pl.CostEstimate(flops=0, bytes_accessed=2 * 1024 * 1024, transcendentals=0),
        name="pack",
    )(slots, queries, cotangent)


def join_kernel(k0_ref, k1_ref, k2_ref, k3_ref, keep_ref, take_ref, kv_ref, n_ref):
    for k, piece in enumerate((k0_ref, k1_ref, k2_ref, k3_ref)):
        kv_ref[k] = piece[...]
    n_ref[:, 0:BLOCK] = keep_ref[...]
    n_ref[:, BLOCK:] = take_ref[...]


def join(kv, keep, take):
    return pl.pallas_call(
        join_kernel,
        out_shape=(
            jax.ShapeDtypeStruct((4, BLOCK, 2 * HD), jnp.bfloat16),
            jax.ShapeDtypeStruct((4, 2 * BLOCK, 512), jnp.bfloat16),
        ),
        in_specs=[VMEM] * 6,
        out_specs=(VMEM, VMEM),
        compiler_params=grant(10),
        cost_estimate=pl.CostEstimate(flops=0, bytes_accessed=2 * 1024 * 1024, transcendentals=0),
        name="join",
    )(*kv, keep, take)


def attend_kernel(
    len_ref, at_ref, a_ref, kv0_ref, kv1_ref, kv2_ref, kv3_ref,
    o_ref, d0_ref, d1_ref, d2_ref, d3_ref, kv_ref, kt_ref, vt_ref, acc_ref,
):
    tiles = SEQ // TILE
    z = at_ref[0]
    y = at_ref[1]
    for a, piece in enumerate((kv0_ref, kv1_ref, kv2_ref, kv3_ref)):
        for k in range(4):
            kv_ref[((z + 4 - k) & 3) * 4 + ((y + 4 - a) & 3)] = piece[k]
    for t in range(tiles):
        kv = kv_ref[2 * t : 2 * t + 2].reshape(TILE, 2 * HD)
        kt_ref[t] = kv[:, :HD].T
        vt_ref[t] = kv[:, HD:].T
    acc_ref[...] = jnp.zeros_like(acc_ref)

    def tile_step(i, carry):
        base = i * TILE
        ends = []
        total = jnp.int32(0)
        for d in range(DOCS):
            total = total + len_ref[0, d]
            ends.append(total)
        first = jnp.int32(0)
        for end in ends:
            first = jnp.where(end <= base, end, first)
        first_tile = first // TILE
        count = i - first_tile + 1
        q_pos = base + lax.broadcasted_iota(jnp.int32, (1, TILE), 1)
        q_start = jnp.zeros((1, TILE), jnp.int32)
        for end in ends:
            q_start = jnp.where(end <= q_pos, end, q_start)
        down = lax.broadcasted_iota(jnp.int32, (TILE, TILE), 0)

        def work(n):
            q = a_ref[pl.ds(2 * i, 2), 0:BLOCK, :].reshape(TILE, HD)
            places = a_ref[pl.ds(2 * i, 2), 2 * BLOCK : 2 * BLOCK + 16, :].astype(jnp.float32)
            place = jnp.concatenate([places[0, 0:1], places[1, 0:1]], axis=1)
            onehot = (down == place.astype(jnp.int32)).astype(jnp.bfloat16)
            g_bal = a_ref[:, pl.ds(pl.multiple_of(BLOCK + 16 * i, 16), 16), :].reshape(TILE, HD)
            gt32 = dot32(g_bal.T, onehot)
            gt = gt32.astype(jnp.bfloat16)
            g = gt.T
            scores = []
            for j in range(n):
                tile = first_tile + j
                key = kv_ref[pl.ds(2 * tile, 2), :, 0:HD].reshape(TILE, HD)
                raw = dot32(key, q, NT)
                k_pos = tile * TILE + down
                seen = k_pos >= q_start
                if j == n - 1:
                    seen = seen & (k_pos <= q_pos)
                scores.append(jnp.where(seen, raw, jnp.float32(-1e30)))
            peak = scores[0]
            for s in scores[1:]:
                peak = jnp.maximum(peak, s)
            peak = jnp.max(peak, axis=0, keepdims=True)
            expo = [jnp.exp2((s - peak) * (SCALE * math.log2(math.e))) for s in scores]
            norm = expo[0]
            for e in expo[1:]:
                norm = norm + e
            inv = 1.0 / jnp.sum(norm, axis=0, keepdims=True)
            prob = [e * inv for e in expo]
            prob16 = [p.astype(jnp.bfloat16) for p in prob]
            out_t = jnp.zeros((HD, TILE), jnp.float32)
            for j in range(n):
                out_t = out_t + dot32(vt_ref[first_tile + j], prob16[j])
            delta = jnp.sum(gt32 * out_t, axis=0, keepdims=True)
            out_bal = dot32(onehot, out_t.astype(jnp.bfloat16), NT).astype(jnp.bfloat16)
            o_ref[:, pl.ds(pl.multiple_of(16 * i, 16), 16), :] = out_bal.reshape(16, 16, HD)
            dq_t = jnp.zeros((HD, TILE), jnp.float32)
            for j in range(n):
                tile = first_tile + j
                value = kv_ref[pl.ds(2 * tile, 2), :, HD : 2 * HD].reshape(TILE, HD)
                grad_prob = dot32(value, g, NT)
                grad_score = (prob[j] * (grad_prob - delta) * SCALE).astype(jnp.bfloat16)
                dq_t = dq_t + dot32(kt_ref[tile], grad_score)
                acc_ref[pl.ds(2 * tile, 2), :, 0:HD] += dot32(grad_score, q).reshape(2, BLOCK, HD)
                acc_ref[pl.ds(2 * tile, 2), :, HD : 2 * HD] += dot32(prob16[j], g).reshape(
                    2, BLOCK, HD
                )
            o_ref[pl.ds(2 * i, 2), BLOCK : 2 * BLOCK, :] = (
                dq_t.astype(jnp.bfloat16).T.reshape(2, BLOCK, HD)
            )

        for n in range(1, MAXTILES + 1):
            pl.when(count == n)(lambda n=n: work(n))
        return carry

    lax.fori_loop(0, tiles, tile_step, 0)
    for a, piece in enumerate((d0_ref, d1_ref, d2_ref, d3_ref)):
        for k in range(4):
            piece[k] = acc_ref[((z + 4 - k) & 3) * 4 + ((y + a) & 3)].astype(piece.dtype)


def attend(lengths, place, rows, kv):
    ways = rows.shape[0]
    tiles = SEQ // TILE
    piece = (4, BLOCK, 2 * HD)
    return pl.pallas_call(
        attend_kernel,
        out_shape=(
            jax.ShapeDtypeStruct((ways, 2 * BLOCK, HD), jnp.bfloat16),
            jax.ShapeDtypeStruct(piece, jnp.float32),
            jax.ShapeDtypeStruct(piece, jnp.bfloat16),
            jax.ShapeDtypeStruct(piece, jnp.bfloat16),
            jax.ShapeDtypeStruct(piece, jnp.bfloat16),
        ),
        in_specs=[SMEM, SMEM] + [VMEM] * 5,
        out_specs=(VMEM,) * 5,
        scratch_shapes=[
            pltpu.VMEM((ways, BLOCK, 2 * HD), jnp.bfloat16),
            pltpu.VMEM((tiles, HD, TILE), jnp.bfloat16),
            pltpu.VMEM((tiles, HD, TILE), jnp.bfloat16),
            pltpu.VMEM((ways, BLOCK, 2 * HD), jnp.float32),
        ],
        compiler_params=grant(22),
        cost_estimate=pl.CostEstimate(
            flops=12 * 2 * SEQ * 640 * HD, bytes_accessed=6 * 1024 * 1024, transcendentals=SEQ * 640
        ),
        name="attend",
    )(lengths, place, rows, *kv)


def weigh_kernel(
    at_ref, m_ref, t_ref, n0_ref, n1_ref, n2_ref, n3_ref,
    w0_ref, w1_ref, w2_ref, w3_ref, d_ref,
):
    for k in range(4):
        d_ref[k, :, 0:BLOCK] = m_ref[k].T
        d_ref[k, :, BLOCK:] = t_ref[k].T
    for a, o_ref in enumerate((w0_ref, w1_ref, w2_ref, w3_ref)):
        chunk = (at_ref[2] + a) & 3
        total = dot32(d_ref[0], n0_ref[chunk])
        total = total + dot32(d_ref[1], n1_ref[chunk])
        total = total + dot32(d_ref[2], n2_ref[chunk])
        total = total + dot32(d_ref[3], n3_ref[chunk])
        o_ref[...] = total.astype(o_ref.dtype)


def weigh(place, mine, theirs, blocks):
    piece = (2 * HD, 512)
    return pl.pallas_call(
        weigh_kernel,
        out_shape=(jax.ShapeDtypeStruct(piece, jnp.float32),)
        + (jax.ShapeDtypeStruct(piece, jnp.bfloat16),) * 3,
        in_specs=[SMEM] + [VMEM] * 6,
        out_specs=(VMEM,) * 4,
        scratch_shapes=[pltpu.VMEM((4, 2 * HD, 2 * BLOCK), jnp.bfloat16)],
        compiler_params=grant(14),
        cost_estimate=pl.CostEstimate(
            flops=2 * 2 * HD * 2048 * 1024, bytes_accessed=6 * 1024 * 1024, transcendentals=0
        ),
        name="weigh",
    )(place, mine, theirs, *blocks)


def settle_kernel(d0_ref, d1_ref, d2_ref, d3_ref, n1_ref, n2_ref, n3_ref, o_ref):
    total = d0_ref[...] + d1_ref[...].astype(jnp.float32)
    total = total + d2_ref[...].astype(jnp.float32) + d3_ref[...].astype(jnp.float32)
    o_ref[...] = total.astype(jnp.bfloat16)


def settle(pieces, after):
    return pl.pallas_call(
        settle_kernel,
        out_shape=jax.ShapeDtypeStruct(pieces[0].shape, jnp.bfloat16),
        in_specs=[VMEM] * 4 + [ANY] * 3,
        out_specs=VMEM,
        compiler_params=grant(6),
        cost_estimate=pl.CostEstimate(flops=0, bytes_accessed=2 * 1024 * 1024, transcendentals=0),
        name="settle",
    )(*pieces, *after)


def tie_kernel(v_ref, after_ref, o_ref):
    pass


def tie(v, after):
    return pl.pallas_call(
        tie_kernel,
        out_shape=jax.ShapeDtypeStruct(v.shape, v.dtype),
        in_specs=[ANY, ANY],
        out_specs=ANY,
        input_output_aliases={0: 0},
        compiler_params=grant(1),
        name="tie",
    )(v, after)


def heads_kernel(at_ref, r0_ref, r1_ref, r2_ref, r3_ref, o_ref, head_ref):
    for k, piece in enumerate((r0_ref, r1_ref, r2_ref, r3_ref)):
        head_ref[(at_ref[0] + k) & 3] = piece[...]
    for h in range(4):
        o_ref[:, h * HD : (h + 1) * HD] = head_ref[h, :, 0:HD]
        o_ref[:, (h + 4) * HD : (h + 5) * HD] = head_ref[h, :, HD:]


def heads_side_by_side(place, pieces):
    return pl.pallas_call(
        heads_kernel,
        out_shape=jax.ShapeDtypeStruct((BLOCK, 8 * HD), jnp.bfloat16),
        in_specs=[SMEM] + [VMEM] * 4,
        out_specs=VMEM,
        scratch_shapes=[pltpu.VMEM((4, BLOCK, 2 * HD), jnp.bfloat16)],
        compiler_params=grant(4),
        cost_estimate=pl.CostEstimate(flops=0, bytes_accessed=512 * 1024, transcendentals=0),
        name="heads",
    )(place, *pieces)


def fold_kernel(w0_ref, w1_ref, w2_ref, w3_ref, o_ref):
    total = w0_ref[...] + w1_ref[...].astype(jnp.float32)
    total = total + w2_ref[...].astype(jnp.float32) + w3_ref[...].astype(jnp.float32)
    o_ref[...] = total.T.astype(jnp.bfloat16).reshape(o_ref.shape)


def fold(pieces):
    return pl.pallas_call(
        fold_kernel,
        out_shape=jax.ShapeDtypeStruct((16, 32, 2 * HD), jnp.bfloat16),
        in_specs=[VMEM] * 4,
        out_specs=VMEM,
        compiler_params=grant(8),
        cost_estimate=pl.CostEstimate(flops=0, bytes_accessed=2 * 1024 * 1024, transcendentals=0),
        name="fold",
    )(*pieces)


def close_kernel(p_ref, o_ref):
    for h in range(4):
        total = p_ref[4 * h].astype(jnp.float32)
        for s in range(1, 4):
            total = total + p_ref[4 * h + s].astype(jnp.float32)
        o_ref[:, h * HD : (h + 1) * HD] = total[:, :HD]
        o_ref[:, (h + 4) * HD : (h + 5) * HD] = total[:, HD:]


def close(parts):
    return pl.pallas_call(
        close_kernel,
        out_shape=jax.ShapeDtypeStruct((32, 8 * HD), jnp.float32),
        in_specs=[VMEM],
        out_specs=VMEM,
        compiler_params=grant(4),
        name="close",
    )(parts)


def unpack_kernel(p_ref, after_ref, out_ref, grad_ref):
    for h in range(HEADS):
        out_ref[:, h * HD : (h + 1) * HD] = p_ref[h, 0:BLOCK]
        grad_ref[:, h * HD : (h + 1) * HD] = p_ref[h, BLOCK:]


def unpack(back, after):
    whole = jax.ShapeDtypeStruct((BLOCK, HEADS * HD), jnp.bfloat16)
    return pl.pallas_call(
        unpack_kernel,
        out_shape=(whole, whole),
        in_specs=[VMEM, ANY],
        out_specs=(VMEM, VMEM),
        compiler_params=grant(8),
        cost_estimate=pl.CostEstimate(flops=0, bytes_accessed=2 * 1024 * 1024, transcendentals=0),
        name="unpack",
    )(back, after)


def shift(v, axis, k):
    return lax.ppermute(v, axis, [(s, (s + k) % 4) for s in range(4)])


def swap(v):
    return lax.ppermute(v, "core", [(0, 1), (1, 0)])


def per_device(normed, queries, cotangent, lengths, balanced_slot, kv_weight):
    x, core, z, y = (lax.axis_index(name) for name in ("x", "core", "z", "y"))
    place = jnp.stack([z, y, x, core]).astype(jnp.int32)
    rows = pack(balanced_slot, queries[0], cotangent[0])
    *mine, keep, give = project(place, normed[0], kv_weight, rows)

    kv = [mine[0]] + [shift(mine[k], "z", k) for k in (1, 2, 3)]
    rows = lax.all_to_all(rows, CTX, 0, 0, tiled=True)
    kv, tokens = join(kv, keep, swap(give))
    kv = [kv] + [shift(kv, "y", k) for k in (1, 2, 3)]
    left = shift(tokens, "z", 1)
    right = shift(tokens, "z", -1)
    across = shift(tokens, "z", 2)

    out, *dkv = attend(lengths, place, rows, kv)

    dkv = [dkv[0]] + [shift(dkv[k], "y", k) for k in (1, 2, 3)]
    dkv = settle(dkv, (left, across, right))
    theirs = swap(dkv)
    back = lax.all_to_all(tie(out, theirs), CTX, 0, 0, tiled=True)

    pieces = weigh(place, dkv, theirs, (tokens, left, across, right))
    own = tie(dkv, pieces[1])
    folded = fold([pieces[0]] + [shift(pieces[k], "x", k) for k in (1, 2, 3)])
    folded = tie(folded, back)
    weight_grad = close(lax.all_to_all(folded, CTX, 0, 0, tiled=True))

    kv_grad = heads_side_by_side(place, [own[0]] + [shift(own[k], "z", -k) for k in (1, 2, 3)])
    input_grad = lax.dot_general(
        kv_grad, kv_weight, NT, preferred_element_type=jnp.float32
    ).astype(jnp.bfloat16)
    attn_out, q_grad = unpack(back, folded)
    return (attn_out[None], q_grad[None], input_grad[None], weight_grad)


def solution(mesh):
    fine = Mesh(mesh.devices.reshape(4, 2, 4, 4), ("x", "core", "z", "y"))
    dp = ("x", "core")
    placed = (
        P(dp, CTX, None),
        P(dp, CTX, None),
        P(dp, CTX, None),
        P(dp, None),
        P(dp, CTX),
        P(),
    )
    return jax.shard_map(
        per_device,
        mesh=fine,
        in_specs=placed,
        out_specs=(
            P(dp, CTX, None),
            P(dp, CTX, None),
            P(dp, CTX, None),
            P(dp + CTX, None),
        ),
        check_vma=False,
    )
```

```python
import math

import jax
import jax.numpy as jnp
from jax import lax
from jax.experimental import pallas as pl
from jax.experimental.pallas import tpu as pltpu
from jax.sharding import Mesh
from jax.sharding import PartitionSpec as P

HD = 128
BLOCK = 128
TILE = 256
SEQ = 2048
DOCS = 8
MAXTILES = 5
SCALE = HD ** (-0.5)
HEADS = 16
CTX = ("z", "y")
VMEM = pl.BlockSpec(memory_space=pltpu.VMEM)
SMEM = pl.BlockSpec(memory_space=pltpu.SMEM)
HBM = pl.BlockSpec(memory_space=pltpu.HBM)
ANY = pl.BlockSpec(memory_space=pl.ANY)
NN = (((1,), (0,)), ((), ()))
NT = (((1,), (1,)), ((), ()))


def grant(mib):
    return pltpu.CompilerParams(vmem_limit_bytes=mib * 1024 * 1024)


def dot32(a, b, dims=NN):
    return lax.dot_general(a, b, dims, preferred_element_type=jnp.float32)


def project_kernel(
    at_ref, x_hbm, w_hbm, after_ref, o0_hbm, o1_hbm, o2_hbm, o3_hbm, keep_hbm, give_hbm,
    x_ref, w_ref, head_ref, x_sem, w_sem, out_sem, col_sem,
):
    steps = w_ref.shape[0]
    width = w_ref.shape[1]
    whole = pltpu.make_async_copy(x_hbm, x_ref, x_sem)
    weights = [
        pltpu.make_async_copy(w_hbm.at[pl.ds(s * width, width)], w_ref.at[s], w_sem.at[s])
        for s in range(steps)
    ]
    whole.start()
    for copy in weights:
        copy.start()
    whole.wait()
    columns = []
    for c in range(4):
        for other, o_hbm in enumerate((keep_hbm, give_hbm)):
            half = at_ref[3] if other == 0 else 1 - at_ref[3]
            start = pl.multiple_of(c * 1024 + half * 512, 512)
            columns.append(
                pltpu.make_async_copy(
                    x_ref.at[:, pl.ds(start, 512)], o_hbm.at[c], col_sem.at[2 * c + other]
                )
            )
    total = jnp.zeros((BLOCK, 8 * HD), jnp.float32)
    for s in range(steps):
        weights[s].wait()
        total = total + dot32(x_ref[:, s * width : (s + 1) * width], w_ref[s])
    for h in range(4):
        head_ref[h, :, 0:HD] = total[:, h * HD : (h + 1) * HD].astype(jnp.bfloat16)
        head_ref[h, :, HD:] = total[:, (h + 4) * HD : (h + 5) * HD].astype(jnp.bfloat16)
    out = [
        pltpu.make_async_copy(head_ref.at[(at_ref[0] + k) & 3], o_hbm, out_sem.at[k])
        for k, o_hbm in enumerate((o0_hbm, o1_hbm, o2_hbm, o3_hbm))
    ]
    for copy in out + columns:
        copy.start()
    for copy in out + columns:
        copy.wait()


def project(place, inputs, weight, after):
    width = inputs.shape[1]
    chunk = 512
    piece = jax.ShapeDtypeStruct((BLOCK, 2 * HD), jnp.bfloat16)
    half = jax.ShapeDtypeStruct((4, BLOCK, 512), jnp.bfloat16)
    return pl.pallas_call(
        project_kernel,
        out_shape=(piece,) * 4 + (half, half),
        in_specs=[SMEM, HBM, HBM, ANY],
        out_specs=(HBM,) * 6,
        scratch_shapes=[
            pltpu.VMEM(inputs.shape, jnp.bfloat16),
            pltpu.VMEM((width // chunk, chunk, 8 * HD), jnp.bfloat16),
            pltpu.VMEM((4, BLOCK, 2 * HD), jnp.bfloat16),
            pltpu.SemaphoreType.DMA,
            pltpu.SemaphoreType.DMA((width // chunk,)),
            pltpu.SemaphoreType.DMA((4,)),
            pltpu.SemaphoreType.DMA((8,)),
        ],
        compiler_params=grant(58),
        cost_estimate=pl.CostEstimate(
            flops=2 * BLOCK * width * 8 * HD, bytes_accessed=14 * 1024 * 1024, transcendentals=0
        ),
        name="project",
    )(place, inputs, weight, after)


def pack_kernel(slot_ref, q_ref, g_ref, rows_ref):
    slots = slot_ref[0:1, :]
    place = ((slots >> 7) * 16 + (slots & 15)).astype(jnp.float32)
    place = jnp.broadcast_to(place, (16, BLOCK)).astype(jnp.bfloat16)
    for h in range(HEADS):
        rows_ref[h, 0:BLOCK] = q_ref[:, h * HD : (h + 1) * HD]
        rows_ref[h, BLOCK : 2 * BLOCK] = g_ref[:, h * HD : (h + 1) * HD]
        rows_ref[h, 2 * BLOCK :] = place


def pack(slots, queries, cotangent):
    return pl.pallas_call(
        pack_kernel,
        out_shape=jax.ShapeDtypeStruct((HEADS, 2 * BLOCK + 16, HD), jnp.bfloat16),
        in_specs=[VMEM] * 3,
        out_specs=VMEM,
        compiler_params=grant(58),
        cost_estimate=pl.CostEstimate(flops=0, bytes_accessed=2 * 1024 * 1024, transcendentals=0),
        name="pack",
    )(slots, queries, cotangent)


def join_kernel(keep_ref, take_ref, n_ref, sem):
    copies = [
        pltpu.make_async_copy(v_ref, n_ref.at[:, pl.ds(i * BLOCK, BLOCK)], sem.at[i])
        for i, v_ref in enumerate((keep_ref, take_ref))
    ]
    for copy in copies:
        copy.start()
    for copy in copies:
        copy.wait()


def join(keep, take):
    return pl.pallas_call(
        join_kernel,
        out_shape=jax.ShapeDtypeStruct((4, 2 * BLOCK, 512), jnp.bfloat16),
        in_specs=[ANY] * 2,
        out_specs=ANY,
        scratch_shapes=[pltpu.SemaphoreType.DMA((2,))],
        compiler_params=grant(4),
        cost_estimate=pl.CostEstimate(flops=0, bytes_accessed=2 * 1024 * 1024, transcendentals=0),
        name="join",
    )(keep, take)


def pile_kernel(at_ref, k0_ref, k1_ref, k2_ref, k3_ref, after_ref, kv_ref):
    for k, piece in enumerate((k0_ref, k1_ref, k2_ref, k3_ref)):
        kv_ref[(at_ref[0] + 4 - k) & 3] = piece[...]


def pile(place, kv, after):
    return pl.pallas_call(
        pile_kernel,
        out_shape=jax.ShapeDtypeStruct((4, BLOCK, 2 * HD), jnp.bfloat16),
        in_specs=[SMEM] + [VMEM] * 4 + [ANY],
        out_specs=VMEM,
        compiler_params=grant(4),
        cost_estimate=pl.CostEstimate(flops=0, bytes_accessed=512 * 1024, transcendentals=0),
        name="pile",
    )(place, *kv, after)


def attend_kernel(
    len_ref, at_ref, a_ref, kv0_ref, kv1_ref, kv2_ref, kv3_ref,
    o_ref, d0_ref, d1_ref, d2_ref, d3_ref, kv_ref, kt_ref, vt_ref, acc_ref, kv_sem,
):
    tiles = SEQ // TILE
    z = at_ref[0]
    y = at_ref[1]
    copies = [
        pltpu.make_async_copy(piece, kv_ref.at[:, (y + 4 - a) & 3], kv_sem.at[a])
        for a, piece in enumerate((kv0_ref, kv1_ref, kv2_ref, kv3_ref))
    ]
    for copy in copies:
        copy.start()
    acc_ref[...] = jnp.zeros_like(acc_ref)
    for copy in copies:
        copy.wait()
    for t in range(tiles):
        kv = kv_ref[t // 2, t % 2 * 2 : t % 2 * 2 + 2].reshape(TILE, 2 * HD)
        kt_ref[t] = kv[:, :HD].T
        vt_ref[t] = kv[:, HD:].T

    def tile_step(i, carry):
        base = i * TILE
        ends = []
        total = jnp.int32(0)
        for d in range(DOCS):
            total = total + len_ref[0, d]
            ends.append(total)
        first = jnp.int32(0)
        for end in ends:
            first = jnp.where(end <= base, end, first)
        first_tile = first // TILE
        count = i - first_tile + 1
        q_pos = base + lax.broadcasted_iota(jnp.int32, (1, TILE), 1)
        q_start = jnp.zeros((1, TILE), jnp.int32)
        for end in ends:
            q_start = jnp.where(end <= q_pos, end, q_start)
        down = lax.broadcasted_iota(jnp.int32, (TILE, TILE), 0)

        def work(n):
            q = a_ref[pl.ds(2 * i, 2), 0:BLOCK, :].reshape(TILE, HD)
            places = a_ref[pl.ds(2 * i, 2), 2 * BLOCK : 2 * BLOCK + 16, :].astype(jnp.float32)
            place = jnp.concatenate([places[0, 0:1], places[1, 0:1]], axis=1)
            onehot = (down == place.astype(jnp.int32)).astype(jnp.bfloat16)
            g_bal = a_ref[:, pl.ds(pl.multiple_of(BLOCK + 16 * i, 16), 16), :].reshape(TILE, HD)
            gt32 = dot32(g_bal.T, onehot)
            gt = gt32.astype(jnp.bfloat16)
            g = gt.T
            scores = []
            for j in range(n):
                tile = first_tile + j
                key = kv_ref[tile >> 1, pl.ds((tile & 1) * 2, 2), :, 0:HD].reshape(TILE, HD)
                raw = dot32(key, q, NT)
                k_pos = tile * TILE + down
                seen = k_pos >= q_start
                if j == n - 1:
                    seen = seen & (k_pos <= q_pos)
                scores.append(jnp.where(seen, raw, jnp.float32(-1e30)))
            peak = scores[0]
            for s in scores[1:]:
                peak = jnp.maximum(peak, s)
            peak = jnp.max(peak, axis=0, keepdims=True)
            expo = [jnp.exp2((s - peak) * (SCALE * math.log2(math.e))) for s in scores]
            norm = expo[0]
            for e in expo[1:]:
                norm = norm + e
            inv = 1.0 / jnp.sum(norm, axis=0, keepdims=True)
            prob = [e * inv for e in expo]
            prob16 = [p.astype(jnp.bfloat16) for p in prob]
            out_t = jnp.zeros((HD, TILE), jnp.float32)
            for j in range(n):
                out_t = out_t + dot32(vt_ref[first_tile + j], prob16[j])
            delta = jnp.sum(gt32 * out_t, axis=0, keepdims=True)
            out_bal = dot32(onehot, out_t.astype(jnp.bfloat16), NT).astype(jnp.bfloat16)
            o_ref[:, pl.ds(pl.multiple_of(16 * i, 16), 16), :] = out_bal.reshape(16, 16, HD)
            dq_t = jnp.zeros((HD, TILE), jnp.float32)
            for j in range(n):
                tile = first_tile + j
                value = kv_ref[tile >> 1, pl.ds((tile & 1) * 2, 2), :, HD : 2 * HD].reshape(TILE, HD)
                grad_prob = dot32(value, g, NT)
                grad_score = (prob[j] * (grad_prob - delta) * SCALE).astype(jnp.bfloat16)
                dq_t = dq_t + dot32(kt_ref[tile], grad_score)
                acc_ref[pl.ds(2 * tile, 2), :, 0:HD] += dot32(grad_score, q).reshape(2, BLOCK, HD)
                acc_ref[pl.ds(2 * tile, 2), :, HD : 2 * HD] += dot32(prob16[j], g).reshape(
                    2, BLOCK, HD
                )
            o_ref[pl.ds(2 * i, 2), BLOCK : 2 * BLOCK, :] = (
                dq_t.astype(jnp.bfloat16).T.reshape(2, BLOCK, HD)
            )

        for n in range(1, MAXTILES + 1):
            pl.when(count == n)(lambda n=n: work(n))
        return carry

    lax.fori_loop(0, tiles, tile_step, 0)
    for a, piece in enumerate((d0_ref, d1_ref, d2_ref, d3_ref)):
        for k in range(4):
            piece[k] = acc_ref[((z + 4 - k) & 3) * 4 + ((y + a) & 3)].astype(piece.dtype)


def attend(lengths, place, rows, kv):
    ways = rows.shape[0]
    tiles = SEQ // TILE
    piece = (4, BLOCK, 2 * HD)
    return pl.pallas_call(
        attend_kernel,
        out_shape=(
            jax.ShapeDtypeStruct((ways, 2 * BLOCK + 64, HD), jnp.bfloat16),
            jax.ShapeDtypeStruct(piece, jnp.float32),
            jax.ShapeDtypeStruct(piece, jnp.bfloat16),
            jax.ShapeDtypeStruct(piece, jnp.bfloat16),
            jax.ShapeDtypeStruct(piece, jnp.bfloat16),
        ),
        in_specs=[SMEM, SMEM, VMEM] + [ANY] * 4,
        out_specs=(VMEM,) * 5,
        scratch_shapes=[
            pltpu.VMEM((4, 4, BLOCK, 2 * HD), jnp.bfloat16),
            pltpu.VMEM((tiles, HD, TILE), jnp.bfloat16),
            pltpu.VMEM((tiles, HD, TILE), jnp.bfloat16),
            pltpu.VMEM((ways, BLOCK, 2 * HD), jnp.float32),
            pltpu.SemaphoreType.DMA((4,)),
        ],
        compiler_params=grant(14),
        cost_estimate=pl.CostEstimate(
            flops=12 * 2 * SEQ * 640 * HD, bytes_accessed=6 * 1024 * 1024, transcendentals=SEQ * 640
        ),
        name="attend",
    )(lengths, place, rows, *kv)


def weigh_kernel(
    at_ref, m_ref, t_ref, n0_ref, n1_ref, n2_ref, n3_ref,
    w0_ref, w1_ref, w2_ref, w3_ref, d_ref,
):
    for k in range(4):
        d_ref[k, :, 0:BLOCK] = m_ref[k].T
        d_ref[k, :, BLOCK:] = t_ref[k].T
    for a, o_ref in enumerate((w0_ref, w1_ref, w2_ref, w3_ref)):
        chunk = (at_ref[2] + a) & 3
        total = dot32(d_ref[0], n0_ref[chunk])
        total = total + dot32(d_ref[1], n1_ref[chunk])
        total = total + dot32(d_ref[2], n2_ref[chunk])
        total = total + dot32(d_ref[3], n3_ref[chunk])
        o_ref[...] = total.astype(o_ref.dtype)


def weigh(place, mine, theirs, blocks):
    piece = (2 * HD, 512)
    return pl.pallas_call(
        weigh_kernel,
        out_shape=(jax.ShapeDtypeStruct(piece, jnp.float32),)
        + (jax.ShapeDtypeStruct(piece, jnp.bfloat16),) * 3,
        in_specs=[SMEM] + [VMEM] * 6,
        out_specs=(VMEM,) * 4,
        scratch_shapes=[
            pltpu.VMEM((4, 2 * HD, 2 * BLOCK), jnp.bfloat16),
        ],
        compiler_params=grant(14),
        cost_estimate=pl.CostEstimate(
            flops=2 * 2 * HD * 2048 * 1024, bytes_accessed=6 * 1024 * 1024, transcendentals=0
        ),
        name="weigh",
    )(place, mine, theirs, *blocks)


def settle_kernel(d0_ref, d1_ref, d2_ref, d3_ref, n1_ref, n2_ref, n3_ref, o_ref):
    total = d0_ref[...] + d1_ref[...].astype(jnp.float32)
    total = total + d2_ref[...].astype(jnp.float32) + d3_ref[...].astype(jnp.float32)
    o_ref[...] = total.astype(jnp.bfloat16)


def settle(pieces, after):
    return pl.pallas_call(
        settle_kernel,
        out_shape=jax.ShapeDtypeStruct(pieces[0].shape, jnp.bfloat16),
        in_specs=[VMEM] * 4 + [ANY] * 3,
        out_specs=VMEM,
        compiler_params=grant(6),
        cost_estimate=pl.CostEstimate(flops=0, bytes_accessed=2 * 1024 * 1024, transcendentals=0),
        name="settle",
    )(*pieces, *after)


def tie_kernel(v_ref, after_ref, o_ref):
    pass


def tie(v, after):
    return pl.pallas_call(
        tie_kernel,
        out_shape=jax.ShapeDtypeStruct(v.shape, v.dtype),
        in_specs=[ANY, ANY],
        out_specs=ANY,
        input_output_aliases={0: 0},
        compiler_params=grant(1),
        name="tie",
    )(v, after)


def heads_kernel(at_ref, r0_ref, r1_ref, r2_ref, r3_ref, o_ref, head_ref):
    for k, piece in enumerate((r0_ref, r1_ref, r2_ref, r3_ref)):
        head_ref[(at_ref[0] + k) & 3] = piece[...]
    for h in range(4):
        o_ref[:, h * HD : (h + 1) * HD] = head_ref[h, :, 0:HD]
        o_ref[:, (h + 4) * HD : (h + 5) * HD] = head_ref[h, :, HD:]


def heads_side_by_side(place, pieces):
    return pl.pallas_call(
        heads_kernel,
        out_shape=jax.ShapeDtypeStruct((BLOCK, 8 * HD), jnp.bfloat16),
        in_specs=[SMEM] + [VMEM] * 4,
        out_specs=VMEM,
        scratch_shapes=[pltpu.VMEM((4, BLOCK, 2 * HD), jnp.bfloat16)],
        compiler_params=grant(4),
        cost_estimate=pl.CostEstimate(flops=0, bytes_accessed=512 * 1024, transcendentals=0),
        name="heads",
    )(place, *pieces)


def fold_kernel(
    w0_ref, w1_ref, w2_ref, w3_ref, rows_ref, after_ref, o_ref, part_ref, sem
):
    total = w0_ref[...] + w1_ref[...].astype(jnp.float32)
    total = total + w2_ref[...].astype(jnp.float32) + w3_ref[...].astype(jnp.float32)
    total = total.T.astype(jnp.bfloat16)
    part_ref[:, 0:32] = total[:, :HD].reshape(HEADS, 32, HD)
    part_ref[:, 32:64] = total[:, HD:].reshape(HEADS, 32, HD)
    copy = pltpu.make_async_copy(part_ref, o_ref.at[:, pl.ds(2 * BLOCK, 64)], sem)
    copy.start()
    copy.wait()


def fold(pieces, rows, after):
    return pl.pallas_call(
        fold_kernel,
        out_shape=jax.ShapeDtypeStruct(rows.shape, rows.dtype),
        in_specs=[VMEM] * 4 + [ANY] * 2,
        out_specs=ANY,
        input_output_aliases={4: 0},
        scratch_shapes=[
            pltpu.VMEM((HEADS, 64, HD), jnp.bfloat16),
            pltpu.SemaphoreType.DMA,
        ],
        compiler_params=grant(8),
        cost_estimate=pl.CostEstimate(flops=0, bytes_accessed=2 * 1024 * 1024, transcendentals=0),
        name="fold",
    )(*pieces, rows, after)


def close_kernel(p_ref, out_ref, grad_ref, weight_ref):
    for h in range(HEADS):
        out_ref[:, h * HD : (h + 1) * HD] = p_ref[h, 0:BLOCK]
        grad_ref[:, h * HD : (h + 1) * HD] = p_ref[h, BLOCK : 2 * BLOCK]
    for h in range(4):
        total = p_ref[4 * h, 2 * BLOCK :].astype(jnp.float32)
        for s in range(1, 4):
            total = total + p_ref[4 * h + s, 2 * BLOCK :].astype(jnp.float32)
        weight_ref[:, h * HD : (h + 1) * HD] = total[:32]
        weight_ref[:, (h + 4) * HD : (h + 5) * HD] = total[32:]


def close(parts):
    whole = jax.ShapeDtypeStruct((BLOCK, HEADS * HD), jnp.bfloat16)
    return pl.pallas_call(
        close_kernel,
        out_shape=(whole, whole, jax.ShapeDtypeStruct((32, 8 * HD), jnp.float32)),
        in_specs=[VMEM],
        out_specs=(VMEM,) * 3,
        compiler_params=grant(8),
        cost_estimate=pl.CostEstimate(flops=0, bytes_accessed=2 * 1024 * 1024, transcendentals=0),
        name="close",
    )(parts)


def shift(v, axis, k):
    return lax.ppermute(v, axis, [(s, (s + k) % 4) for s in range(4)])


def swap(v):
    return lax.ppermute(v, "core", [(0, 1), (1, 0)])


def per_device(normed, queries, cotangent, lengths, balanced_slot, kv_weight):
    x, core, z, y = (lax.axis_index(name) for name in ("x", "core", "z", "y"))
    place = jnp.stack([z, y, x, core]).astype(jnp.int32)
    rows = pack(balanced_slot, queries[0], cotangent[0])
    *mine, keep, give = project(place, normed[0], kv_weight, rows)

    kv = [mine[0]] + [shift(mine[k], "z", k) for k in (1, 2, 3)]
    rows = lax.all_to_all(rows, CTX, 0, 0, tiled=True)
    tokens = join(keep, swap(give))
    kv = pile(place, kv, tokens)
    kv = [kv] + [shift(kv, "y", k) for k in (1, 2, 3)]
    left = shift(tokens, "z", 1)
    right = shift(tokens, "z", -1)
    across = shift(tokens, "z", 2)

    out, *dkv = attend(lengths, place, rows, kv)

    dkv = [dkv[0]] + [shift(dkv[k], "y", k) for k in (1, 2, 3)]
    dkv = settle(dkv, (left, across, right))
    theirs = swap(dkv)

    pieces = weigh(place, dkv, theirs, (tokens, left, across, right))
    sums = [shift(pieces[k], "x", k) for k in (1, 2, 3)]
    own = tie(dkv, sums[0])

    kv_grad = heads_side_by_side(place, [own[0]] + [shift(own[k], "z", -k) for k in (1, 2, 3)])
    input_grad = lax.dot_general(
        kv_grad, kv_weight, NT, preferred_element_type=jnp.float32
    ).astype(jnp.bfloat16)
    parts = lax.all_to_all(fold([pieces[0]] + sums, out, kv_grad), CTX, 0, 0, tiled=True)
    attn_out, q_grad, weight_grad = close(parts)
    return (attn_out[None], q_grad[None], input_grad[None], weight_grad)


def solution(mesh):
    fine = Mesh(mesh.devices.reshape(4, 2, 4, 4), ("x", "core", "z", "y"))
    dp = ("x", "core")
    placed = (
        P(dp, CTX, None),
        P(dp, CTX, None),
        P(dp, CTX, None),
        P(dp, None),
        P(dp, CTX),
        P(),
    )
    return jax.shard_map(
        per_device,
        mesh=fine,
        in_specs=placed,
        out_specs=(
            P(dp, CTX, None),
            P(dp, CTX, None),
            P(dp, CTX, None),
            P(dp + CTX, None),
        ),
        check_vma=False,
    )
```

```python
import math

import jax
import jax.numpy as jnp
from jax import lax
from jax.experimental import pallas as pl
from jax.experimental.pallas import tpu as pltpu
from jax.sharding import Mesh
from jax.sharding import PartitionSpec as P

HD = 128
BLOCK = 128
TILE = 256
SEQ = 2048
DOCS = 8
MAXTILES = 5
SCALE = HD ** (-0.5)
HEADS = 16
CTX = ("z", "y")
VMEM = pl.BlockSpec(memory_space=pltpu.VMEM)
SMEM = pl.BlockSpec(memory_space=pltpu.SMEM)
HBM = pl.BlockSpec(memory_space=pltpu.HBM)
ANY = pl.BlockSpec(memory_space=pl.ANY)
NN = (((1,), (0,)), ((), ()))
NT = (((1,), (1,)), ((), ()))


def grant(mib):
    return pltpu.CompilerParams(vmem_limit_bytes=mib * 1024 * 1024)


def dot32(a, b, dims=NN):
    return lax.dot_general(a, b, dims, preferred_element_type=jnp.float32)


def project_kernel(
    at_ref, x_hbm, w_hbm, after_ref, o0_hbm, o1_hbm, o2_hbm, o3_hbm, keep_hbm, give_hbm,
    x_ref, w_ref, head_ref, x_sem, w_sem, out_sem, col_sem,
):
    steps = w_ref.shape[0]
    width = w_ref.shape[1]
    whole = pltpu.make_async_copy(x_hbm, x_ref, x_sem)
    weights = [
        pltpu.make_async_copy(w_hbm.at[pl.ds(s * width, width)], w_ref.at[s], w_sem.at[s])
        for s in range(steps)
    ]
    whole.start()
    for copy in weights:
        copy.start()
    whole.wait()
    columns = []
    for c in range(4):
        for other, o_hbm in enumerate((keep_hbm, give_hbm)):
            half = at_ref[3] if other == 0 else 1 - at_ref[3]
            start = pl.multiple_of(c * 1024 + half * 512, 512)
            columns.append(
                pltpu.make_async_copy(
                    x_ref.at[:, pl.ds(start, 512)], o_hbm.at[c], col_sem.at[2 * c + other]
                )
            )
    total = jnp.zeros((BLOCK, 8 * HD), jnp.float32)
    for s in range(steps):
        weights[s].wait()
        total = total + dot32(x_ref[:, s * width : (s + 1) * width], w_ref[s])
    for h in range(4):
        head_ref[h, :, 0:HD] = total[:, h * HD : (h + 1) * HD].astype(jnp.bfloat16)
        head_ref[h, :, HD:] = total[:, (h + 4) * HD : (h + 5) * HD].astype(jnp.bfloat16)
    out = [
        pltpu.make_async_copy(head_ref.at[(at_ref[0] + k) & 3], o_hbm, out_sem.at[k])
        for k, o_hbm in enumerate((o0_hbm, o1_hbm, o2_hbm, o3_hbm))
    ]
    for copy in out + columns:
        copy.start()
    for copy in out + columns:
        copy.wait()


def project(place, inputs, weight, after):
    width = inputs.shape[1]
    chunk = 512
    piece = jax.ShapeDtypeStruct((BLOCK, 2 * HD), jnp.bfloat16)
    half = jax.ShapeDtypeStruct((4, BLOCK, 512), jnp.bfloat16)
    return pl.pallas_call(
        project_kernel,
        out_shape=(piece,) * 4 + (half, half),
        in_specs=[SMEM, HBM, HBM, ANY],
        out_specs=(HBM,) * 6,
        scratch_shapes=[
            pltpu.VMEM(inputs.shape, jnp.bfloat16),
            pltpu.VMEM((width // chunk, chunk, 8 * HD), jnp.bfloat16),
            pltpu.VMEM((4, BLOCK, 2 * HD), jnp.bfloat16),
            pltpu.SemaphoreType.DMA,
            pltpu.SemaphoreType.DMA((width // chunk,)),
            pltpu.SemaphoreType.DMA((4,)),
            pltpu.SemaphoreType.DMA((8,)),
        ],
        compiler_params=grant(58),
        cost_estimate=pl.CostEstimate(
            flops=2 * BLOCK * width * 8 * HD, bytes_accessed=14 * 1024 * 1024, transcendentals=0
        ),
        name="project",
    )(place, inputs, weight, after)


def pack_kernel(slot_ref, q_ref, g_ref, rows_ref):
    slots = slot_ref[0:1, :]
    place = ((slots >> 7) * 16 + (slots & 15)).astype(jnp.float32)
    place = jnp.broadcast_to(place, (16, BLOCK)).astype(jnp.bfloat16)
    for h in range(HEADS):
        rows_ref[h, 0:BLOCK] = q_ref[:, h * HD : (h + 1) * HD]
        rows_ref[h, BLOCK : 2 * BLOCK] = g_ref[:, h * HD : (h + 1) * HD]
        rows_ref[h, 2 * BLOCK :] = place


def pack(slots, queries, cotangent):
    return pl.pallas_call(
        pack_kernel,
        out_shape=jax.ShapeDtypeStruct((HEADS, 2 * BLOCK + 16, HD), jnp.bfloat16),
        in_specs=[VMEM] * 3,
        out_specs=VMEM,
        compiler_params=grant(58),
        cost_estimate=pl.CostEstimate(flops=0, bytes_accessed=2 * 1024 * 1024, transcendentals=0),
        name="pack",
    )(slots, queries, cotangent)


def join_kernel(keep_ref, take_ref, n_ref, sem):
    copies = [
        pltpu.make_async_copy(v_ref, n_ref.at[:, pl.ds(i * BLOCK, BLOCK)], sem.at[i])
        for i, v_ref in enumerate((keep_ref, take_ref))
    ]
    for copy in copies:
        copy.start()
    for copy in copies:
        copy.wait()


def join(keep, take):
    return pl.pallas_call(
        join_kernel,
        out_shape=jax.ShapeDtypeStruct((4, 2 * BLOCK, 512), jnp.bfloat16),
        in_specs=[ANY] * 2,
        out_specs=ANY,
        scratch_shapes=[pltpu.SemaphoreType.DMA((2,))],
        compiler_params=grant(4),
        cost_estimate=pl.CostEstimate(flops=0, bytes_accessed=2 * 1024 * 1024, transcendentals=0),
        name="join",
    )(keep, take)


def pile_kernel(at_ref, k0_ref, k1_ref, k2_ref, k3_ref, after_ref, kv_ref):
    for k, piece in enumerate((k0_ref, k1_ref, k2_ref, k3_ref)):
        kv_ref[(at_ref[0] + 4 - k) & 3] = piece[...]


def pile(place, kv, after):
    return pl.pallas_call(
        pile_kernel,
        out_shape=jax.ShapeDtypeStruct((4, BLOCK, 2 * HD), jnp.bfloat16),
        in_specs=[SMEM] + [VMEM] * 4 + [ANY],
        out_specs=VMEM,
        compiler_params=grant(4),
        cost_estimate=pl.CostEstimate(flops=0, bytes_accessed=512 * 1024, transcendentals=0),
        name="pile",
    )(place, *kv, after)


def attend_kernel(
    len_ref, at_ref, a_ref, kv0_ref, kv1_ref, kv2_ref, kv3_ref,
    o_ref, d0_ref, d1_ref, d2_ref, d3_ref, kv_ref, kt_ref, vt_ref, acc_ref, kv_sem,
):
    tiles = SEQ // TILE
    z = at_ref[0]
    y = at_ref[1]
    copies = [
        pltpu.make_async_copy(piece, kv_ref.at[:, (y + 4 - a) & 3], kv_sem.at[a])
        for a, piece in enumerate((kv0_ref, kv1_ref, kv2_ref, kv3_ref))
    ]
    for copy in copies:
        copy.start()
    acc_ref[...] = jnp.zeros_like(acc_ref)
    for copy in copies:
        copy.wait()
    for t in range(tiles):
        kv = kv_ref[t // 2, t % 2 * 2 : t % 2 * 2 + 2].reshape(TILE, 2 * HD)
        kt_ref[t] = kv[:, :HD].T
        vt_ref[t] = kv[:, HD:].T

    def tile_step(i, carry):
        base = i * TILE
        ends = []
        total = jnp.int32(0)
        for d in range(DOCS):
            total = total + len_ref[0, d]
            ends.append(total)
        first = jnp.int32(0)
        for end in ends:
            first = jnp.where(end <= base, end, first)
        first_tile = first // TILE
        count = i - first_tile + 1
        q_pos = base + lax.broadcasted_iota(jnp.int32, (1, TILE), 1)
        q_start = jnp.zeros((1, TILE), jnp.int32)
        for end in ends:
            q_start = jnp.where(end <= q_pos, end, q_start)
        down = lax.broadcasted_iota(jnp.int32, (TILE, TILE), 0)

        def work(n):
            q = a_ref[pl.ds(2 * i, 2), 0:BLOCK, :].reshape(TILE, HD)
            places = a_ref[pl.ds(2 * i, 2), 2 * BLOCK : 2 * BLOCK + 16, :].astype(jnp.float32)
            place = jnp.concatenate([places[0, 0:1], places[1, 0:1]], axis=1)
            onehot = (down == place.astype(jnp.int32)).astype(jnp.bfloat16)
            g_bal = a_ref[:, pl.ds(pl.multiple_of(BLOCK + 16 * i, 16), 16), :].reshape(TILE, HD)
            gt32 = dot32(g_bal.T, onehot)
            gt = gt32.astype(jnp.bfloat16)
            g = gt.T
            scores = []
            for j in range(n):
                tile = first_tile + j
                key = kv_ref[tile >> 1, pl.ds((tile & 1) * 2, 2), :, 0:HD].reshape(TILE, HD)
                raw = dot32(key, q, NT)
                k_pos = tile * TILE + down
                seen = k_pos >= q_start
                if j == n - 1:
                    seen = seen & (k_pos <= q_pos)
                scores.append(jnp.where(seen, raw, jnp.float32(-1e30)))
            peak = scores[0]
            for s in scores[1:]:
                peak = jnp.maximum(peak, s)
            peak = jnp.max(peak, axis=0, keepdims=True)
            expo = [jnp.exp2((s - peak) * (SCALE * math.log2(math.e))) for s in scores]
            norm = expo[0]
            for e in expo[1:]:
                norm = norm + e
            inv = 1.0 / jnp.sum(norm, axis=0, keepdims=True)
            prob = [e * inv for e in expo]
            prob16 = [p.astype(jnp.bfloat16) for p in prob]
            out_t = jnp.zeros((HD, TILE), jnp.float32)
            for j in range(n):
                out_t = out_t + dot32(vt_ref[first_tile + j], prob16[j])
            delta = jnp.sum(gt32 * out_t, axis=0, keepdims=True)
            out_bal = dot32(onehot, out_t.astype(jnp.bfloat16), NT).astype(jnp.bfloat16)
            o_ref[:, pl.ds(pl.multiple_of(16 * i, 16), 16), :] = out_bal.reshape(16, 16, HD)
            dq_t = jnp.zeros((HD, TILE), jnp.float32)
            for j in range(n):
                tile = first_tile + j
                value = kv_ref[tile >> 1, pl.ds((tile & 1) * 2, 2), :, HD : 2 * HD].reshape(TILE, HD)
                grad_prob = dot32(value, g, NT)
                grad_score = (prob[j] * (grad_prob - delta) * SCALE).astype(jnp.bfloat16)
                dq_t = dq_t + dot32(kt_ref[tile], grad_score)
                acc_ref[pl.ds(2 * tile, 2), :, 0:HD] += dot32(grad_score, q).reshape(2, BLOCK, HD)
                acc_ref[pl.ds(2 * tile, 2), :, HD : 2 * HD] += dot32(prob16[j], g).reshape(
                    2, BLOCK, HD
                )
            o_ref[pl.ds(2 * i, 2), BLOCK : 2 * BLOCK, :] = (
                dq_t.astype(jnp.bfloat16).T.reshape(2, BLOCK, HD)
            )

        for n in range(1, MAXTILES + 1):
            pl.when(count == n)(lambda n=n: work(n))
        return carry

    lax.fori_loop(0, tiles, tile_step, 0)
    for a, piece in enumerate((d0_ref, d1_ref, d2_ref, d3_ref)):
        for k in range(4):
            piece[k] = acc_ref[((z + 4 - k) & 3) * 4 + ((y + a) & 3)].astype(piece.dtype)


def attend(lengths, place, rows, kv):
    ways = rows.shape[0]
    tiles = SEQ // TILE
    piece = (4, BLOCK, 2 * HD)
    return pl.pallas_call(
        attend_kernel,
        out_shape=(
            jax.ShapeDtypeStruct((ways, 2 * BLOCK + 64, HD), jnp.bfloat16),
            jax.ShapeDtypeStruct(piece, jnp.float32),
            jax.ShapeDtypeStruct(piece, jnp.bfloat16),
            jax.ShapeDtypeStruct(piece, jnp.bfloat16),
            jax.ShapeDtypeStruct(piece, jnp.bfloat16),
        ),
        in_specs=[SMEM, SMEM, VMEM] + [ANY] * 4,
        out_specs=(VMEM,) * 5,
        scratch_shapes=[
            pltpu.VMEM((4, 4, BLOCK, 2 * HD), jnp.bfloat16),
            pltpu.VMEM((tiles, HD, TILE), jnp.bfloat16),
            pltpu.VMEM((tiles, HD, TILE), jnp.bfloat16),
            pltpu.VMEM((ways, BLOCK, 2 * HD), jnp.float32),
            pltpu.SemaphoreType.DMA((4,)),
        ],
        compiler_params=grant(14),
        cost_estimate=pl.CostEstimate(
            flops=12 * 2 * SEQ * 640 * HD, bytes_accessed=6 * 1024 * 1024, transcendentals=SEQ * 640
        ),
        name="attend",
    )(lengths, place, rows, *kv)


def weigh_kernel(
    at_ref, m_ref, t_ref, n0_ref, n1_ref, n2_ref, n3_ref,
    w0_ref, w1_ref, w2_ref, w3_ref, d_ref,
):
    for k in range(4):
        d_ref[k, :, 0:BLOCK] = m_ref[k].T
        d_ref[k, :, BLOCK:] = t_ref[k].T
    for a, o_ref in enumerate((w0_ref, w1_ref, w2_ref, w3_ref)):
        chunk = (at_ref[2] + a) & 3
        total = dot32(d_ref[0], n0_ref[chunk])
        total = total + dot32(d_ref[1], n1_ref[chunk])
        total = total + dot32(d_ref[2], n2_ref[chunk])
        total = total + dot32(d_ref[3], n3_ref[chunk])
        o_ref[...] = total.astype(o_ref.dtype)


def weigh(place, mine, theirs, blocks):
    piece = (2 * HD, 512)
    return pl.pallas_call(
        weigh_kernel,
        out_shape=(jax.ShapeDtypeStruct(piece, jnp.float32),)
        + (jax.ShapeDtypeStruct(piece, jnp.bfloat16),) * 3,
        in_specs=[SMEM] + [VMEM] * 6,
        out_specs=(VMEM,) * 4,
        scratch_shapes=[
            pltpu.VMEM((4, 2 * HD, 2 * BLOCK), jnp.bfloat16),
        ],
        compiler_params=grant(14),
        cost_estimate=pl.CostEstimate(
            flops=2 * 2 * HD * 2048 * 1024, bytes_accessed=6 * 1024 * 1024, transcendentals=0
        ),
        name="weigh",
    )(place, mine, theirs, *blocks)


def settle_kernel(d0_ref, d1_ref, d2_ref, d3_ref, n1_ref, n2_ref, n3_ref, o_ref):
    total = d0_ref[...] + d1_ref[...].astype(jnp.float32)
    total = total + d2_ref[...].astype(jnp.float32) + d3_ref[...].astype(jnp.float32)
    o_ref[...] = total.astype(jnp.bfloat16)


def settle(pieces, after):
    return pl.pallas_call(
        settle_kernel,
        out_shape=jax.ShapeDtypeStruct(pieces[0].shape, jnp.bfloat16),
        in_specs=[VMEM] * 4 + [ANY] * 3,
        out_specs=VMEM,
        compiler_params=grant(6),
        cost_estimate=pl.CostEstimate(flops=0, bytes_accessed=2 * 1024 * 1024, transcendentals=0),
        name="settle",
    )(*pieces, *after)


def tie_kernel(v_ref, after_ref, o_ref):
    pass


def tie(v, after):
    return pl.pallas_call(
        tie_kernel,
        out_shape=jax.ShapeDtypeStruct(v.shape, v.dtype),
        in_specs=[ANY, ANY],
        out_specs=ANY,
        input_output_aliases={0: 0},
        compiler_params=grant(1),
        name="tie",
    )(v, after)


def heads_kernel(at_ref, r0_ref, r1_ref, r2_ref, r3_ref, o_ref, head_ref):
    for k, piece in enumerate((r0_ref, r1_ref, r2_ref, r3_ref)):
        head_ref[(at_ref[0] + k) & 3] = piece[...]
    for h in range(4):
        o_ref[:, h * HD : (h + 1) * HD] = head_ref[h, :, 0:HD]
        o_ref[:, (h + 4) * HD : (h + 5) * HD] = head_ref[h, :, HD:]


def heads_side_by_side(place, pieces):
    return pl.pallas_call(
        heads_kernel,
        out_shape=jax.ShapeDtypeStruct((BLOCK, 8 * HD), jnp.bfloat16),
        in_specs=[SMEM] + [VMEM] * 4,
        out_specs=VMEM,
        scratch_shapes=[pltpu.VMEM((4, BLOCK, 2 * HD), jnp.bfloat16)],
        compiler_params=grant(4),
        cost_estimate=pl.CostEstimate(flops=0, bytes_accessed=512 * 1024, transcendentals=0),
        name="heads",
    )(place, *pieces)


def fold_kernel(w0_ref, w1_ref, w2_ref, w3_ref, rows_ref, o_ref, part_ref, sem):
    total = w0_ref[...] + w1_ref[...].astype(jnp.float32)
    total = total + w2_ref[...].astype(jnp.float32) + w3_ref[...].astype(jnp.float32)
    total = total.T.astype(jnp.bfloat16)
    part_ref[:, 0:32] = total[:, :HD].reshape(HEADS, 32, HD)
    part_ref[:, 32:64] = total[:, HD:].reshape(HEADS, 32, HD)
    copy = pltpu.make_async_copy(part_ref, o_ref.at[:, pl.ds(2 * BLOCK, 64)], sem)
    copy.start()
    copy.wait()


def fold(pieces, rows):
    return pl.pallas_call(
        fold_kernel,
        out_shape=jax.ShapeDtypeStruct(rows.shape, rows.dtype),
        in_specs=[VMEM] * 4 + [ANY],
        out_specs=ANY,
        input_output_aliases={4: 0},
        scratch_shapes=[
            pltpu.VMEM((HEADS, 64, HD), jnp.bfloat16),
            pltpu.SemaphoreType.DMA,
        ],
        compiler_params=grant(8),
        cost_estimate=pl.CostEstimate(flops=0, bytes_accessed=2 * 1024 * 1024, transcendentals=0),
        name="fold",
    )(*pieces, rows)


def close_kernel(p_ref, out_ref, grad_ref, weight_ref):
    for h in range(HEADS):
        out_ref[:, h * HD : (h + 1) * HD] = p_ref[h, 0:BLOCK]
        grad_ref[:, h * HD : (h + 1) * HD] = p_ref[h, BLOCK : 2 * BLOCK]
    for h in range(4):
        total = p_ref[4 * h, 2 * BLOCK :].astype(jnp.float32)
        for s in range(1, 4):
            total = total + p_ref[4 * h + s, 2 * BLOCK :].astype(jnp.float32)
        weight_ref[:, h * HD : (h + 1) * HD] = total[:32]
        weight_ref[:, (h + 4) * HD : (h + 5) * HD] = total[32:]


def close(parts):
    whole = jax.ShapeDtypeStruct((BLOCK, HEADS * HD), jnp.bfloat16)
    return pl.pallas_call(
        close_kernel,
        out_shape=(whole, whole, jax.ShapeDtypeStruct((32, 8 * HD), jnp.float32)),
        in_specs=[VMEM],
        out_specs=(VMEM,) * 3,
        compiler_params=grant(8),
        cost_estimate=pl.CostEstimate(flops=0, bytes_accessed=2 * 1024 * 1024, transcendentals=0),
        name="close",
    )(parts)


def shift(v, axis, k):
    return lax.ppermute(v, axis, [(s, (s + k) % 4) for s in range(4)])


def swap(v):
    return lax.ppermute(v, "core", [(0, 1), (1, 0)])


def per_device(normed, queries, cotangent, lengths, balanced_slot, kv_weight):
    x, core, z, y = (lax.axis_index(name) for name in ("x", "core", "z", "y"))
    place = jnp.stack([z, y, x, core]).astype(jnp.int32)
    rows = pack(balanced_slot, queries[0], cotangent[0])
    *mine, keep, give = project(place, normed[0], kv_weight, rows)

    kv = [mine[0]] + [shift(mine[k], "z", k) for k in (1, 2, 3)]
    rows = lax.all_to_all(rows, CTX, 0, 0, tiled=True)
    tokens = join(keep, swap(give))
    kv = pile(place, kv, tokens)
    kv = [kv] + [shift(kv, "y", k) for k in (1, 2, 3)]
    left = shift(tokens, "z", 1)
    right = shift(tokens, "z", -1)
    across = shift(tokens, "z", 2)

    out, *dkv = attend(lengths, place, rows, kv)

    dkv = [dkv[0]] + [shift(dkv[k], "y", k) for k in (1, 2, 3)]
    dkv = settle(dkv, (left, across, right))
    theirs = swap(dkv)

    pieces = weigh(place, dkv, theirs, (tokens, left, across, right))
    sums = [shift(pieces[k], "x", k) for k in (1, 2, 3)]
    own = tie(dkv, pieces[1])

    kv_grad = heads_side_by_side(place, [own[0]] + [shift(own[k], "z", -k) for k in (1, 2, 3)])
    input_grad = lax.dot_general(
        kv_grad, kv_weight, NT, preferred_element_type=jnp.float32
    ).astype(jnp.bfloat16)
    parts = lax.all_to_all(fold([pieces[0]] + sums, out), CTX, 0, 0, tiled=True)
    attn_out, q_grad, weight_grad = close(parts)
    return (attn_out[None], q_grad[None], input_grad[None], weight_grad)


def solution(mesh):
    fine = Mesh(mesh.devices.reshape(4, 2, 4, 4), ("x", "core", "z", "y"))
    dp = ("x", "core")
    placed = (
        P(dp, CTX, None),
        P(dp, CTX, None),
        P(dp, CTX, None),
        P(dp, None),
        P(dp, CTX),
        P(),
    )
    return jax.shard_map(
        per_device,
        mesh=fine,
        in_specs=placed,
        out_specs=(
            P(dp, CTX, None),
            P(dp, CTX, None),
            P(dp, CTX, None),
            P(dp + CTX, None),
        ),
        check_vma=False,
    )
```

```python
import math

import jax
import jax.numpy as jnp
from jax import lax
from jax.experimental import pallas as pl
from jax.experimental.pallas import tpu as pltpu
from jax.sharding import Mesh
from jax.sharding import PartitionSpec as P

HD = 128
BLOCK = 128
TILE = 256
SEQ = 2048
DOCS = 8
MAXTILES = 5
SCALE = HD ** (-0.5)
HEADS = 16
CTX = ("z", "y")
VMEM = pl.BlockSpec(memory_space=pltpu.VMEM)
SMEM = pl.BlockSpec(memory_space=pltpu.SMEM)
HBM = pl.BlockSpec(memory_space=pltpu.HBM)
ANY = pl.BlockSpec(memory_space=pl.ANY)
NN = (((1,), (0,)), ((), ()))
NT = (((1,), (1,)), ((), ()))


def grant(mib):
    return pltpu.CompilerParams(vmem_limit_bytes=mib * 1024 * 1024)


def dot32(a, b, dims=NN):
    return lax.dot_general(a, b, dims, preferred_element_type=jnp.float32)


def project_kernel(
    at_ref, x_hbm, w_hbm, after_ref, o0_hbm, o1_hbm, o2_hbm, o3_hbm, keep_hbm, give_hbm,
    x_ref, w_ref, head_ref, x_sem, w_sem, out_sem, col_sem,
):
    steps = w_ref.shape[0]
    width = w_ref.shape[1]
    whole = pltpu.make_async_copy(x_hbm, x_ref, x_sem)
    weights = [
        pltpu.make_async_copy(w_hbm.at[pl.ds(s * width, width)], w_ref.at[s], w_sem.at[s])
        for s in range(steps)
    ]
    whole.start()
    for copy in weights:
        copy.start()
    whole.wait()
    columns = []
    for c in range(4):
        for other, o_hbm in enumerate((keep_hbm, give_hbm)):
            half = at_ref[3] if other == 0 else 1 - at_ref[3]
            start = pl.multiple_of(c * 1024 + half * 512, 512)
            columns.append(
                pltpu.make_async_copy(
                    x_ref.at[:, pl.ds(start, 512)], o_hbm.at[c], col_sem.at[2 * c + other]
                )
            )
    total = jnp.zeros((BLOCK, 8 * HD), jnp.float32)
    for s in range(steps):
        weights[s].wait()
        total = total + dot32(x_ref[:, s * width : (s + 1) * width], w_ref[s])
    for h in range(4):
        head_ref[h, :, 0:HD] = total[:, h * HD : (h + 1) * HD].astype(jnp.bfloat16)
        head_ref[h, :, HD:] = total[:, (h + 4) * HD : (h + 5) * HD].astype(jnp.bfloat16)
    out = [
        pltpu.make_async_copy(head_ref.at[(at_ref[0] + k) & 3], o_hbm, out_sem.at[k])
        for k, o_hbm in enumerate((o0_hbm, o1_hbm, o2_hbm, o3_hbm))
    ]
    for copy in out + columns:
        copy.start()
    for copy in out + columns:
        copy.wait()


def project(place, inputs, weight, after):
    width = inputs.shape[1]
    chunk = 512
    piece = jax.ShapeDtypeStruct((BLOCK, 2 * HD), jnp.bfloat16)
    half = jax.ShapeDtypeStruct((4, BLOCK, 512), jnp.bfloat16)
    return pl.pallas_call(
        project_kernel,
        out_shape=(piece,) * 4 + (half, half),
        in_specs=[SMEM, HBM, HBM, ANY],
        out_specs=(HBM,) * 6,
        scratch_shapes=[
            pltpu.VMEM(inputs.shape, jnp.bfloat16),
            pltpu.VMEM((width // chunk, chunk, 8 * HD), jnp.bfloat16),
            pltpu.VMEM((4, BLOCK, 2 * HD), jnp.bfloat16),
            pltpu.SemaphoreType.DMA,
            pltpu.SemaphoreType.DMA((width // chunk,)),
            pltpu.SemaphoreType.DMA((4,)),
            pltpu.SemaphoreType.DMA((8,)),
        ],
        compiler_params=grant(58),
        cost_estimate=pl.CostEstimate(
            flops=2 * BLOCK * width * 8 * HD, bytes_accessed=14 * 1024 * 1024, transcendentals=0
        ),
        name="project",
    )(place, inputs, weight, after)


def pack_kernel(slot_ref, q_ref, g_ref, rows_ref):
    slots = slot_ref[0:1, :]
    place = ((slots >> 7) * 16 + (slots & 15)).astype(jnp.float32)
    place = jnp.broadcast_to(place, (16, BLOCK)).astype(jnp.bfloat16)
    for h in range(HEADS):
        rows_ref[h, 0:BLOCK] = q_ref[:, h * HD : (h + 1) * HD]
        rows_ref[h, BLOCK : 2 * BLOCK] = g_ref[:, h * HD : (h + 1) * HD]
        rows_ref[h, 2 * BLOCK :] = place


def pack(slots, queries, cotangent):
    return pl.pallas_call(
        pack_kernel,
        out_shape=jax.ShapeDtypeStruct((HEADS, 2 * BLOCK + 16, HD), jnp.bfloat16),
        in_specs=[VMEM, VMEM, VMEM],
        out_specs=VMEM,
        compiler_params=grant(58),
        cost_estimate=pl.CostEstimate(flops=0, bytes_accessed=2 * 1024 * 1024, transcendentals=0),
        name="pack",
    )(slots, queries, cotangent)


def join_kernel(keep_ref, take_ref, n_ref, sem):
    copies = [
        pltpu.make_async_copy(v_ref, n_ref.at[:, pl.ds(i * BLOCK, BLOCK)], sem.at[i])
        for i, v_ref in enumerate((keep_ref, take_ref))
    ]
    for copy in copies:
        copy.start()
    for copy in copies:
        copy.wait()


def join(keep, take):
    return pl.pallas_call(
        join_kernel,
        out_shape=jax.ShapeDtypeStruct((4, 2 * BLOCK, 512), jnp.bfloat16),
        in_specs=[ANY] * 2,
        out_specs=ANY,
        scratch_shapes=[pltpu.SemaphoreType.DMA((2,))],
        compiler_params=grant(4),
        cost_estimate=pl.CostEstimate(flops=0, bytes_accessed=2 * 1024 * 1024, transcendentals=0),
        name="join",
    )(keep, take)


def pile_kernel(k0_ref, k1_ref, k2_ref, k3_ref, after_ref, kv_ref):
    for k, piece in enumerate((k0_ref, k1_ref, k2_ref, k3_ref)):
        kv_ref[k] = piece[...]


def pile(kv, after):
    return pl.pallas_call(
        pile_kernel,
        out_shape=jax.ShapeDtypeStruct((4, BLOCK, 2 * HD), jnp.bfloat16),
        in_specs=[VMEM] * 4 + [ANY],
        out_specs=VMEM,
        compiler_params=grant(4),
        cost_estimate=pl.CostEstimate(flops=0, bytes_accessed=512 * 1024, transcendentals=0),
        name="pile",
    )(*kv, after)


def attend_kernel(
    len_ref, at_ref, a_ref, kv0_ref, kv1_ref, kv2_ref, kv3_ref,
    o_ref, d0_ref, d1_ref, d2_ref, d3_ref, kv_ref, kt_ref, vt_ref, acc_ref,
):
    tiles = SEQ // TILE
    z = at_ref[0]
    y = at_ref[1]
    for a, piece in enumerate((kv0_ref, kv1_ref, kv2_ref, kv3_ref)):
        for k in range(4):
            kv_ref[((z + 4 - k) & 3) * 4 + ((y + 4 - a) & 3)] = piece[k]
    acc_ref[...] = jnp.zeros_like(acc_ref)
    for t in range(tiles):
        kv = kv_ref[2 * t : 2 * t + 2].reshape(TILE, 2 * HD)
        kt_ref[t] = kv[:, :HD].T
        vt_ref[t] = kv[:, HD:].T

    def tile_step(i, carry):
        base = i * TILE
        ends = []
        total = jnp.int32(0)
        for d in range(DOCS):
            total = total + len_ref[0, d]
            ends.append(total)
        first = jnp.int32(0)
        for end in ends:
            first = jnp.where(end <= base, end, first)
        first_tile = first // TILE
        count = i - first_tile + 1
        q_pos = base + lax.broadcasted_iota(jnp.int32, (1, TILE), 1)
        q_start = jnp.zeros((1, TILE), jnp.int32)
        for end in ends:
            q_start = jnp.where(end <= q_pos, end, q_start)
        down = lax.broadcasted_iota(jnp.int32, (TILE, TILE), 0)

        def work(n):
            q = a_ref[pl.ds(2 * i, 2), 0:BLOCK, :].reshape(TILE, HD)
            places = a_ref[pl.ds(2 * i, 2), 2 * BLOCK : 2 * BLOCK + 16, :].astype(jnp.float32)
            place = jnp.concatenate([places[0, 0:1], places[1, 0:1]], axis=1)
            onehot = (down == place.astype(jnp.int32)).astype(jnp.bfloat16)
            g_bal = a_ref[:, pl.ds(pl.multiple_of(BLOCK + 16 * i, 16), 16), :].reshape(TILE, HD)
            gt32 = dot32(g_bal.T, onehot)
            gt = gt32.astype(jnp.bfloat16)
            g = gt.T
            scores = []
            for j in range(n):
                tile = first_tile + j
                key = kv_ref[pl.ds(2 * tile, 2), :, 0:HD].reshape(TILE, HD)
                raw = dot32(key, q, NT)
                k_pos = tile * TILE + down
                seen = k_pos >= q_start
                if j == n - 1:
                    seen = seen & (k_pos <= q_pos)
                scores.append(jnp.where(seen, raw, jnp.float32(-1e30)))
            peak = scores[0]
            for s in scores[1:]:
                peak = jnp.maximum(peak, s)
            peak = jnp.max(peak, axis=0, keepdims=True)
            expo = [jnp.exp2((s - peak) * (SCALE * math.log2(math.e))) for s in scores]
            norm = expo[0]
            for e in expo[1:]:
                norm = norm + e
            inv = 1.0 / jnp.sum(norm, axis=0, keepdims=True)
            prob = [e * inv for e in expo]
            prob16 = [p.astype(jnp.bfloat16) for p in prob]
            out_t = jnp.zeros((HD, TILE), jnp.float32)
            for j in range(n):
                out_t = out_t + dot32(vt_ref[first_tile + j], prob16[j])
            delta = jnp.sum(gt32 * out_t, axis=0, keepdims=True)
            out_bal = dot32(onehot, out_t.astype(jnp.bfloat16), NT).astype(jnp.bfloat16)
            o_ref[:, pl.ds(pl.multiple_of(16 * i, 16), 16), :] = out_bal.reshape(16, 16, HD)
            dq_t = jnp.zeros((HD, TILE), jnp.float32)
            for j in range(n):
                tile = first_tile + j
                value = kv_ref[pl.ds(2 * tile, 2), :, HD : 2 * HD].reshape(TILE, HD)
                grad_prob = dot32(value, g, NT)
                grad_score = (prob[j] * (grad_prob - delta) * SCALE).astype(jnp.bfloat16)
                dq_t = dq_t + dot32(kt_ref[tile], grad_score)
                acc_ref[pl.ds(2 * tile, 2), :, 0:HD] += dot32(grad_score, q).reshape(2, BLOCK, HD)
                acc_ref[pl.ds(2 * tile, 2), :, HD : 2 * HD] += dot32(prob16[j], g).reshape(
                    2, BLOCK, HD
                )
            o_ref[pl.ds(2 * i, 2), BLOCK : 2 * BLOCK, :] = (
                dq_t.astype(jnp.bfloat16).T.reshape(2, BLOCK, HD)
            )

        for n in range(1, MAXTILES + 1):
            pl.when(count == n)(lambda n=n: work(n))
        return carry

    lax.fori_loop(0, tiles, tile_step, 0)
    for a, piece in enumerate((d0_ref, d1_ref, d2_ref, d3_ref)):
        for k in range(4):
            piece[k] = acc_ref[((z + 4 - k) & 3) * 4 + ((y + a) & 3)].astype(piece.dtype)


def attend(lengths, place, rows, kv):
    ways = rows.shape[0]
    tiles = SEQ // TILE
    piece = (4, BLOCK, 2 * HD)
    return pl.pallas_call(
        attend_kernel,
        out_shape=(
            jax.ShapeDtypeStruct((ways, 2 * BLOCK, HD), jnp.bfloat16),
            jax.ShapeDtypeStruct(piece, jnp.float32),
            jax.ShapeDtypeStruct(piece, jnp.bfloat16),
            jax.ShapeDtypeStruct(piece, jnp.bfloat16),
            jax.ShapeDtypeStruct(piece, jnp.bfloat16),
        ),
        in_specs=[SMEM, SMEM] + [VMEM] * 5,
        out_specs=(VMEM,) * 5,
        scratch_shapes=[
            pltpu.VMEM((ways, BLOCK, 2 * HD), jnp.bfloat16),
            pltpu.VMEM((tiles, HD, TILE), jnp.bfloat16),
            pltpu.VMEM((tiles, HD, TILE), jnp.bfloat16),
            pltpu.VMEM((ways, BLOCK, 2 * HD), jnp.float32),
        ],
        compiler_params=grant(22),
        cost_estimate=pl.CostEstimate(
            flops=12 * 2 * SEQ * 640 * HD, bytes_accessed=6 * 1024 * 1024, transcendentals=SEQ * 640
        ),
        name="attend",
    )(lengths, place, rows, *kv)


def weigh_kernel(
    at_ref, m_ref, t_ref, n0_ref, n1_ref, n2_ref, n3_ref,
    w0_ref, w1_ref, w2_ref, w3_ref, d_ref, n_ref, sem,
):
    copies = [
        pltpu.make_async_copy(v_ref, n_ref.at[k], sem.at[k])
        for k, v_ref in enumerate((n0_ref, n1_ref, n2_ref, n3_ref))
    ]
    for copy in copies:
        copy.start()
    for k in range(4):
        d_ref[k, :, 0:BLOCK] = m_ref[k].T
        d_ref[k, :, BLOCK:] = t_ref[k].T
    for copy in copies:
        copy.wait()
    for a, o_ref in ((1, w1_ref), (3, w3_ref), (2, w2_ref), (0, w0_ref)):
        chunk = (at_ref[2] + a) & 3
        total = dot32(d_ref[0], n_ref[0, chunk])
        for k in range(1, 4):
            total = total + dot32(d_ref[k], n_ref[k, chunk])
        o_ref[...] = total.astype(o_ref.dtype)


def weigh(place, mine, theirs, blocks):
    piece = (2 * HD, 512)
    return pl.pallas_call(
        weigh_kernel,
        out_shape=(jax.ShapeDtypeStruct(piece, jnp.float32),)
        + (jax.ShapeDtypeStruct(piece, jnp.bfloat16),) * 3,
        in_specs=[SMEM] + [VMEM] * 2 + [ANY] * 4,
        out_specs=(VMEM,) * 4,
        scratch_shapes=[
            pltpu.VMEM((4, 2 * HD, 2 * BLOCK), jnp.bfloat16),
            pltpu.VMEM((4, 4, 2 * BLOCK, 512), jnp.bfloat16),
            pltpu.SemaphoreType.DMA((4,)),
        ],
        compiler_params=grant(14),
        cost_estimate=pl.CostEstimate(
            flops=2 * 2 * HD * 2048 * 1024, bytes_accessed=6 * 1024 * 1024, transcendentals=0
        ),
        name="weigh",
    )(place, mine, theirs, *blocks)


def settle_kernel(d0_ref, d1_ref, d2_ref, d3_ref, n1_ref, n2_ref, n3_ref, o_ref):
    total = d0_ref[...] + d1_ref[...].astype(jnp.float32)
    total = total + d2_ref[...].astype(jnp.float32) + d3_ref[...].astype(jnp.float32)
    o_ref[...] = total.astype(jnp.bfloat16)


def settle(pieces, after):
    return pl.pallas_call(
        settle_kernel,
        out_shape=jax.ShapeDtypeStruct(pieces[0].shape, jnp.bfloat16),
        in_specs=[VMEM] * 4 + [ANY] * 3,
        out_specs=VMEM,
        compiler_params=grant(6),
        cost_estimate=pl.CostEstimate(flops=0, bytes_accessed=2 * 1024 * 1024, transcendentals=0),
        name="settle",
    )(*pieces, *after)


def tie_kernel(v_ref, after_ref, o_ref):
    pass


def tie(v, after):
    return pl.pallas_call(
        tie_kernel,
        out_shape=jax.ShapeDtypeStruct(v.shape, v.dtype),
        in_specs=[ANY, ANY],
        out_specs=ANY,
        input_output_aliases={0: 0},
        compiler_params=grant(1),
        name="tie",
    )(v, after)


def heads_kernel(at_ref, r0_ref, r1_ref, r2_ref, r3_ref, o_ref, head_ref):
    for k, piece in enumerate((r0_ref, r1_ref, r2_ref, r3_ref)):
        head_ref[(at_ref[0] + k) & 3] = piece[...]
    for h in range(4):
        o_ref[:, h * HD : (h + 1) * HD] = head_ref[h, :, 0:HD]
        o_ref[:, (h + 4) * HD : (h + 5) * HD] = head_ref[h, :, HD:]


def heads_side_by_side(place, pieces):
    return pl.pallas_call(
        heads_kernel,
        out_shape=jax.ShapeDtypeStruct((BLOCK, 8 * HD), jnp.bfloat16),
        in_specs=[SMEM] + [VMEM] * 4,
        out_specs=VMEM,
        scratch_shapes=[pltpu.VMEM((4, BLOCK, 2 * HD), jnp.bfloat16)],
        compiler_params=grant(4),
        cost_estimate=pl.CostEstimate(flops=0, bytes_accessed=512 * 1024, transcendentals=0),
        name="heads",
    )(place, *pieces)


def fold_kernel(w0_ref, w1_ref, w2_ref, w3_ref, after_ref, o_ref):
    total = w0_ref[...] + w1_ref[...].astype(jnp.float32)
    total = total + w2_ref[...].astype(jnp.float32) + w3_ref[...].astype(jnp.float32)
    o_ref[...] = total.T.astype(jnp.bfloat16).reshape(o_ref.shape)


def fold(pieces, after):
    return pl.pallas_call(
        fold_kernel,
        out_shape=jax.ShapeDtypeStruct((16, 32, 2 * HD), jnp.bfloat16),
        in_specs=[VMEM] * 4 + [ANY],
        out_specs=VMEM,
        compiler_params=grant(8),
        cost_estimate=pl.CostEstimate(flops=0, bytes_accessed=2 * 1024 * 1024, transcendentals=0),
        name="fold",
    )(*pieces, after)


def close_kernel(p_ref, o_ref):
    for h in range(4):
        total = p_ref[4 * h].astype(jnp.float32)
        for s in range(1, 4):
            total = total + p_ref[4 * h + s].astype(jnp.float32)
        o_ref[:, h * HD : (h + 1) * HD] = total[:, :HD]
        o_ref[:, (h + 4) * HD : (h + 5) * HD] = total[:, HD:]


def close(parts):
    return pl.pallas_call(
        close_kernel,
        out_shape=jax.ShapeDtypeStruct((32, 8 * HD), jnp.float32),
        in_specs=[VMEM],
        out_specs=VMEM,
        compiler_params=grant(4),
        name="close",
    )(parts)


def unpack_kernel(p_ref, after_ref, out_ref, grad_ref):
    for h in range(HEADS):
        out_ref[:, h * HD : (h + 1) * HD] = p_ref[h, 0:BLOCK]
        grad_ref[:, h * HD : (h + 1) * HD] = p_ref[h, BLOCK:]


def unpack(back, after):
    whole = jax.ShapeDtypeStruct((BLOCK, HEADS * HD), jnp.bfloat16)
    return pl.pallas_call(
        unpack_kernel,
        out_shape=(whole, whole),
        in_specs=[VMEM, ANY],
        out_specs=(VMEM, VMEM),
        compiler_params=grant(8),
        cost_estimate=pl.CostEstimate(flops=0, bytes_accessed=2 * 1024 * 1024, transcendentals=0),
        name="unpack",
    )(back, after)


def shift(v, axis, k):
    return lax.ppermute(v, axis, [(s, (s + k) % 4) for s in range(4)])


def swap(v):
    return lax.ppermute(v, "core", [(0, 1), (1, 0)])


def per_device(normed, queries, cotangent, lengths, balanced_slot, kv_weight):
    x, core, z, y = (lax.axis_index(name) for name in ("x", "core", "z", "y"))
    place = jnp.stack([z, y, x, core]).astype(jnp.int32)
    rows = pack(balanced_slot, queries[0], cotangent[0])
    *mine, keep, give = project(place, normed[0], kv_weight, rows)

    kv = [mine[0]] + [shift(mine[k], "z", k) for k in (1, 2, 3)]
    rows = lax.all_to_all(rows, CTX, 0, 0, tiled=True)
    tokens = join(keep, swap(give))
    kv = pile(kv, tokens)
    kv = [kv] + [shift(kv, "y", k) for k in (1, 2, 3)]
    left = shift(tokens, "z", 1)
    right = shift(tokens, "z", -1)
    across = shift(tokens, "z", 2)

    out, *dkv = attend(lengths, place, rows, kv)

    dkv = [dkv[0]] + [shift(dkv[k], "y", k) for k in (1, 2, 3)]
    back = lax.all_to_all(tie(out, dkv[1]), CTX, 0, 0, tiled=True)
    dkv = settle(dkv, (left, across, right))
    theirs = swap(dkv)

    pieces = weigh(place, dkv, theirs, (tokens, left, across, right))
    own = tie(dkv, pieces[1])
    pieces = [pieces[0]] + [shift(pieces[k], "x", k) for k in (1, 2, 3)]

    kv_grad = heads_side_by_side(place, [own[0]] + [shift(own[k], "z", -k) for k in (1, 2, 3)])
    input_grad = lax.dot_general(
        kv_grad, kv_weight, NT, preferred_element_type=jnp.float32
    ).astype(jnp.bfloat16)
    folded = tie(fold(pieces, kv_grad), back)
    weight_grad = close(lax.all_to_all(folded, CTX, 0, 0, tiled=True))
    attn_out, q_grad = unpack(back, folded)
    return (attn_out[None], q_grad[None], input_grad[None], weight_grad)


def solution(mesh):
    fine = Mesh(mesh.devices.reshape(4, 2, 4, 4), ("x", "core", "z", "y"))
    dp = ("x", "core")
    placed = (
        P(dp, CTX, None),
        P(dp, CTX, None),
        P(dp, CTX, None),
        P(dp, None),
        P(dp, CTX),
        P(),
    )
    return jax.shard_map(
        per_device,
        mesh=fine,
        in_specs=placed,
        out_specs=(
            P(dp, CTX, None),
            P(dp, CTX, None),
            P(dp, CTX, None),
            P(dp + CTX, None),
        ),
        check_vma=False,
    )
```

```python
import math

import jax
import jax.numpy as jnp
from jax import lax
from jax.experimental import pallas as pl
from jax.experimental.pallas import tpu as pltpu
from jax.sharding import Mesh
from jax.sharding import PartitionSpec as P

HD = 128
BLOCK = 128
TILE = 256
SEQ = 2048
DOCS = 8
MAXTILES = 5
SCALE = HD ** (-0.5)
HEADS = 16
CTX = ("z", "y")
VMEM = pl.BlockSpec(memory_space=pltpu.VMEM)
SMEM = pl.BlockSpec(memory_space=pltpu.SMEM)
HBM = pl.BlockSpec(memory_space=pltpu.HBM)
ANY = pl.BlockSpec(memory_space=pl.ANY)
NN = (((1,), (0,)), ((), ()))
NT = (((1,), (1,)), ((), ()))


def grant(mib):
    return pltpu.CompilerParams(vmem_limit_bytes=mib * 1024 * 1024)


def dot32(a, b, dims=NN):
    return lax.dot_general(a, b, dims, preferred_element_type=jnp.float32)


def project_kernel(
    at_ref, x_hbm, w_hbm, after_ref, o0_hbm, o1_hbm, o2_hbm, o3_hbm, keep_hbm, give_hbm,
    x_ref, w_ref, head_ref, x_sem, w_sem, out_sem, col_sem,
):
    steps = w_ref.shape[0]
    width = w_ref.shape[1]
    whole = pltpu.make_async_copy(x_hbm, x_ref, x_sem)
    weights = [
        pltpu.make_async_copy(w_hbm.at[pl.ds(s * width, width)], w_ref.at[s], w_sem.at[s])
        for s in range(steps)
    ]
    whole.start()
    for copy in weights:
        copy.start()
    whole.wait()
    columns = []
    for c in range(4):
        for other, o_hbm in enumerate((keep_hbm, give_hbm)):
            half = at_ref[3] if other == 0 else 1 - at_ref[3]
            start = pl.multiple_of(c * 1024 + half * 512, 512)
            columns.append(
                pltpu.make_async_copy(
                    x_ref.at[:, pl.ds(start, 512)], o_hbm.at[c], col_sem.at[2 * c + other]
                )
            )
    total = jnp.zeros((BLOCK, 8 * HD), jnp.float32)
    for s in range(steps):
        weights[s].wait()
        total = total + dot32(x_ref[:, s * width : (s + 1) * width], w_ref[s])
    for h in range(4):
        head_ref[h, :, 0:HD] = total[:, h * HD : (h + 1) * HD].astype(jnp.bfloat16)
        head_ref[h, :, HD:] = total[:, (h + 4) * HD : (h + 5) * HD].astype(jnp.bfloat16)
    out = [
        pltpu.make_async_copy(head_ref.at[(at_ref[0] + k) & 3], o_hbm, out_sem.at[k])
        for k, o_hbm in enumerate((o0_hbm, o1_hbm, o2_hbm, o3_hbm))
    ]
    for copy in out + columns:
        copy.start()
    for copy in out + columns:
        copy.wait()


def project(place, inputs, weight, after):
    width = inputs.shape[1]
    chunk = 512
    piece = jax.ShapeDtypeStruct((BLOCK, 2 * HD), jnp.bfloat16)
    half = jax.ShapeDtypeStruct((4, BLOCK, 512), jnp.bfloat16)
    return pl.pallas_call(
        project_kernel,
        out_shape=(piece,) * 4 + (half, half),
        in_specs=[SMEM, HBM, HBM, ANY],
        out_specs=(HBM,) * 6,
        scratch_shapes=[
            pltpu.VMEM(inputs.shape, jnp.bfloat16),
            pltpu.VMEM((width // chunk, chunk, 8 * HD), jnp.bfloat16),
            pltpu.VMEM((4, BLOCK, 2 * HD), jnp.bfloat16),
            pltpu.SemaphoreType.DMA,
            pltpu.SemaphoreType.DMA((width // chunk,)),
            pltpu.SemaphoreType.DMA((4,)),
            pltpu.SemaphoreType.DMA((8,)),
        ],
        compiler_params=grant(58),
        cost_estimate=pl.CostEstimate(
            flops=2 * BLOCK * width * 8 * HD, bytes_accessed=14 * 1024 * 1024, transcendentals=0
        ),
        name="project",
    )(place, inputs, weight, after)


def pack_kernel(slot_ref, q_ref, g_ref, rows_ref):
    slots = slot_ref[0:1, :]
    place = ((slots >> 7) * 16 + (slots & 15)).astype(jnp.float32)
    place = jnp.broadcast_to(place, (16, BLOCK)).astype(jnp.bfloat16)
    for h in range(HEADS):
        rows_ref[h, 0:BLOCK] = q_ref[:, h * HD : (h + 1) * HD]
        rows_ref[h, BLOCK : 2 * BLOCK] = g_ref[:, h * HD : (h + 1) * HD]
        rows_ref[h, 2 * BLOCK :] = place


def pack(slots, queries, cotangent):
    return pl.pallas_call(
        pack_kernel,
        out_shape=jax.ShapeDtypeStruct((HEADS, 2 * BLOCK + 16, HD), jnp.bfloat16),
        in_specs=[VMEM, VMEM, VMEM],
        out_specs=VMEM,
        compiler_params=grant(58),
        cost_estimate=pl.CostEstimate(flops=0, bytes_accessed=2 * 1024 * 1024, transcendentals=0),
        name="pack",
    )(slots, queries, cotangent)


def join_kernel(keep_ref, take_ref, n_ref, sem):
    copies = [
        pltpu.make_async_copy(v_ref, n_ref.at[:, pl.ds(i * BLOCK, BLOCK)], sem.at[i])
        for i, v_ref in enumerate((keep_ref, take_ref))
    ]
    for copy in copies:
        copy.start()
    for copy in copies:
        copy.wait()


def join(keep, take):
    return pl.pallas_call(
        join_kernel,
        out_shape=jax.ShapeDtypeStruct((4, 2 * BLOCK, 512), jnp.bfloat16),
        in_specs=[ANY] * 2,
        out_specs=ANY,
        scratch_shapes=[pltpu.SemaphoreType.DMA((2,))],
        compiler_params=grant(4),
        cost_estimate=pl.CostEstimate(flops=0, bytes_accessed=2 * 1024 * 1024, transcendentals=0),
        name="join",
    )(keep, take)


def pile_kernel(k0_ref, k1_ref, k2_ref, k3_ref, after_ref, kv_ref):
    for k, piece in enumerate((k0_ref, k1_ref, k2_ref, k3_ref)):
        kv_ref[k] = piece[...]


def pile(kv, after):
    return pl.pallas_call(
        pile_kernel,
        out_shape=jax.ShapeDtypeStruct((4, BLOCK, 2 * HD), jnp.bfloat16),
        in_specs=[VMEM] * 4 + [ANY],
        out_specs=VMEM,
        compiler_params=grant(4),
        cost_estimate=pl.CostEstimate(flops=0, bytes_accessed=512 * 1024, transcendentals=0),
        name="pile",
    )(*kv, after)


def attend_kernel(
    len_ref, at_ref, a_ref, kv0_ref, kv1_ref, kv2_ref, kv3_ref,
    o_ref, d0_ref, d1_ref, d2_ref, d3_ref, kv_ref, kt_ref, vt_ref, acc_ref,
):
    tiles = SEQ // TILE
    z = at_ref[0]
    y = at_ref[1]
    for a, piece in enumerate((kv0_ref, kv1_ref, kv2_ref, kv3_ref)):
        for k in range(4):
            kv_ref[((z + 4 - k) & 3) * 4 + ((y + 4 - a) & 3)] = piece[k]
    acc_ref[...] = jnp.zeros_like(acc_ref)
    for t in range(tiles):
        kv = kv_ref[2 * t : 2 * t + 2].reshape(TILE, 2 * HD)
        kt_ref[t] = kv[:, :HD].T
        vt_ref[t] = kv[:, HD:].T

    def tile_step(i, carry):
        base = i * TILE
        ends = []
        total = jnp.int32(0)
        for d in range(DOCS):
            total = total + len_ref[0, d]
            ends.append(total)
        first = jnp.int32(0)
        for end in ends:
            first = jnp.where(end <= base, end, first)
        first_tile = first // TILE
        count = i - first_tile + 1
        q_pos = base + lax.broadcasted_iota(jnp.int32, (1, TILE), 1)
        q_start = jnp.zeros((1, TILE), jnp.int32)
        for end in ends:
            q_start = jnp.where(end <= q_pos, end, q_start)
        down = lax.broadcasted_iota(jnp.int32, (TILE, TILE), 0)

        def work(n):
            q = a_ref[pl.ds(2 * i, 2), 0:BLOCK, :].reshape(TILE, HD)
            places = a_ref[pl.ds(2 * i, 2), 2 * BLOCK : 2 * BLOCK + 16, :].astype(jnp.float32)
            place = jnp.concatenate([places[0, 0:1], places[1, 0:1]], axis=1)
            onehot = (down == place.astype(jnp.int32)).astype(jnp.bfloat16)
            g_bal = a_ref[:, pl.ds(pl.multiple_of(BLOCK + 16 * i, 16), 16), :].reshape(TILE, HD)
            gt32 = dot32(g_bal.T, onehot)
            gt = gt32.astype(jnp.bfloat16)
            g = gt.T
            scores = []
            for j in range(n):
                tile = first_tile + j
                key = kv_ref[pl.ds(2 * tile, 2), :, 0:HD].reshape(TILE, HD)
                raw = dot32(key, q, NT)
                k_pos = tile * TILE + down
                seen = k_pos >= q_start
                if j == n - 1:
                    seen = seen & (k_pos <= q_pos)
                scores.append(jnp.where(seen, raw, jnp.float32(-1e30)))
            peak = scores[0]
            for s in scores[1:]:
                peak = jnp.maximum(peak, s)
            peak = jnp.max(peak, axis=0, keepdims=True)
            expo = [jnp.exp2((s - peak) * (SCALE * math.log2(math.e))) for s in scores]
            norm = expo[0]
            for e in expo[1:]:
                norm = norm + e
            inv = 1.0 / jnp.sum(norm, axis=0, keepdims=True)
            prob = [e * inv for e in expo]
            prob16 = [p.astype(jnp.bfloat16) for p in prob]
            out_t = jnp.zeros((HD, TILE), jnp.float32)
            for j in range(n):
                out_t = out_t + dot32(vt_ref[first_tile + j], prob16[j])
            delta = jnp.sum(gt32 * out_t, axis=0, keepdims=True)
            out_bal = dot32(onehot, out_t.astype(jnp.bfloat16), NT).astype(jnp.bfloat16)
            o_ref[:, pl.ds(pl.multiple_of(16 * i, 16), 16), :] = out_bal.reshape(16, 16, HD)
            dq_t = jnp.zeros((HD, TILE), jnp.float32)
            for j in range(n):
                tile = first_tile + j
                value = kv_ref[pl.ds(2 * tile, 2), :, HD : 2 * HD].reshape(TILE, HD)
                grad_prob = dot32(value, g, NT)
                grad_score = (prob[j] * (grad_prob - delta) * SCALE).astype(jnp.bfloat16)
                dq_t = dq_t + dot32(kt_ref[tile], grad_score)
                acc_ref[pl.ds(2 * tile, 2), :, 0:HD] += dot32(grad_score, q).reshape(2, BLOCK, HD)
                acc_ref[pl.ds(2 * tile, 2), :, HD : 2 * HD] += dot32(prob16[j], g).reshape(
                    2, BLOCK, HD
                )
            o_ref[pl.ds(2 * i, 2), BLOCK : 2 * BLOCK, :] = (
                dq_t.astype(jnp.bfloat16).T.reshape(2, BLOCK, HD)
            )

        for n in range(1, MAXTILES + 1):
            pl.when(count == n)(lambda n=n: work(n))
        return carry

    lax.fori_loop(0, tiles, tile_step, 0)
    for a, piece in enumerate((d0_ref, d1_ref, d2_ref, d3_ref)):
        for k in range(4):
            piece[k] = acc_ref[((z + 4 - k) & 3) * 4 + ((y + a) & 3)].astype(piece.dtype)


def attend(lengths, place, rows, kv):
    ways = rows.shape[0]
    tiles = SEQ // TILE
    piece = (4, BLOCK, 2 * HD)
    return pl.pallas_call(
        attend_kernel,
        out_shape=(
            jax.ShapeDtypeStruct((ways, 2 * BLOCK, HD), jnp.bfloat16),
            jax.ShapeDtypeStruct(piece, jnp.float32),
            jax.ShapeDtypeStruct(piece, jnp.bfloat16),
            jax.ShapeDtypeStruct(piece, jnp.bfloat16),
            jax.ShapeDtypeStruct(piece, jnp.bfloat16),
        ),
        in_specs=[SMEM, SMEM] + [VMEM] * 5,
        out_specs=(VMEM,) * 5,
        scratch_shapes=[
            pltpu.VMEM((ways, BLOCK, 2 * HD), jnp.bfloat16),
            pltpu.VMEM((tiles, HD, TILE), jnp.bfloat16),
            pltpu.VMEM((tiles, HD, TILE), jnp.bfloat16),
            pltpu.VMEM((ways, BLOCK, 2 * HD), jnp.float32),
        ],
        compiler_params=grant(22),
        cost_estimate=pl.CostEstimate(
            flops=12 * 2 * SEQ * 640 * HD, bytes_accessed=6 * 1024 * 1024, transcendentals=SEQ * 640
        ),
        name="attend",
    )(lengths, place, rows, *kv)


def weigh_kernel(
    at_ref, m_ref, t_ref, n0_ref, n1_ref, n2_ref, n3_ref,
    w0_ref, w1_ref, w2_ref, w3_ref, d_ref, n_ref, sem,
):
    copies = [
        pltpu.make_async_copy(v_ref, n_ref.at[k], sem.at[k])
        for k, v_ref in enumerate((n0_ref, n1_ref, n2_ref, n3_ref))
    ]
    for copy in copies:
        copy.start()
    for k in range(4):
        d_ref[k, :, 0:BLOCK] = m_ref[k].T
        d_ref[k, :, BLOCK:] = t_ref[k].T
    for copy in copies:
        copy.wait()
    for a, o_ref in ((1, w1_ref), (3, w3_ref), (2, w2_ref), (0, w0_ref)):
        chunk = (at_ref[2] + a) & 3
        total = dot32(d_ref[0], n_ref[0, chunk])
        for k in range(1, 4):
            total = total + dot32(d_ref[k], n_ref[k, chunk])
        o_ref[...] = total.astype(o_ref.dtype)


def weigh(place, mine, theirs, blocks):
    piece = (2 * HD, 512)
    return pl.pallas_call(
        weigh_kernel,
        out_shape=(jax.ShapeDtypeStruct(piece, jnp.float32),)
        + (jax.ShapeDtypeStruct(piece, jnp.bfloat16),) * 3,
        in_specs=[SMEM] + [VMEM] * 2 + [ANY] * 4,
        out_specs=(VMEM,) * 4,
        scratch_shapes=[
            pltpu.VMEM((4, 2 * HD, 2 * BLOCK), jnp.bfloat16),
            pltpu.VMEM((4, 4, 2 * BLOCK, 512), jnp.bfloat16),
            pltpu.SemaphoreType.DMA((4,)),
        ],
        compiler_params=grant(14),
        cost_estimate=pl.CostEstimate(
            flops=2 * 2 * HD * 2048 * 1024, bytes_accessed=6 * 1024 * 1024, transcendentals=0
        ),
        name="weigh",
    )(place, mine, theirs, *blocks)


def settle_kernel(d0_ref, d1_ref, d2_ref, d3_ref, n1_ref, n2_ref, n3_ref, o_ref):
    total = d0_ref[...] + d1_ref[...].astype(jnp.float32)
    total = total + d2_ref[...].astype(jnp.float32) + d3_ref[...].astype(jnp.float32)
    o_ref[...] = total.astype(jnp.bfloat16)


def settle(pieces, after):
    return pl.pallas_call(
        settle_kernel,
        out_shape=jax.ShapeDtypeStruct(pieces[0].shape, jnp.bfloat16),
        in_specs=[VMEM] * 4 + [ANY] * 3,
        out_specs=VMEM,
        compiler_params=grant(6),
        cost_estimate=pl.CostEstimate(flops=0, bytes_accessed=2 * 1024 * 1024, transcendentals=0),
        name="settle",
    )(*pieces, *after)


def tie_kernel(v_ref, after_ref, o_ref):
    pass


def tie(v, after):
    return pl.pallas_call(
        tie_kernel,
        out_shape=jax.ShapeDtypeStruct(v.shape, v.dtype),
        in_specs=[ANY, ANY],
        out_specs=ANY,
        input_output_aliases={0: 0},
        compiler_params=grant(1),
        name="tie",
    )(v, after)


def heads_kernel(at_ref, r0_ref, r1_ref, r2_ref, r3_ref, o_ref, head_ref):
    for k, piece in enumerate((r0_ref, r1_ref, r2_ref, r3_ref)):
        head_ref[(at_ref[0] + k) & 3] = piece[...]
    for h in range(4):
        o_ref[:, h * HD : (h + 1) * HD] = head_ref[h, :, 0:HD]
        o_ref[:, (h + 4) * HD : (h + 5) * HD] = head_ref[h, :, HD:]


def heads_side_by_side(place, pieces):
    return pl.pallas_call(
        heads_kernel,
        out_shape=jax.ShapeDtypeStruct((BLOCK, 8 * HD), jnp.bfloat16),
        in_specs=[SMEM] + [VMEM] * 4,
        out_specs=VMEM,
        scratch_shapes=[pltpu.VMEM((4, BLOCK, 2 * HD), jnp.bfloat16)],
        compiler_params=grant(4),
        cost_estimate=pl.CostEstimate(flops=0, bytes_accessed=512 * 1024, transcendentals=0),
        name="heads",
    )(place, *pieces)


def fold_kernel(w0_ref, w1_ref, w2_ref, w3_ref, o_ref):
    total = w0_ref[...] + w1_ref[...].astype(jnp.float32)
    total = total + w2_ref[...].astype(jnp.float32) + w3_ref[...].astype(jnp.float32)
    o_ref[...] = total.T.astype(jnp.bfloat16).reshape(o_ref.shape)


def fold(pieces):
    return pl.pallas_call(
        fold_kernel,
        out_shape=jax.ShapeDtypeStruct((16, 32, 2 * HD), jnp.bfloat16),
        in_specs=[VMEM] * 4,
        out_specs=VMEM,
        compiler_params=grant(8),
        cost_estimate=pl.CostEstimate(flops=0, bytes_accessed=2 * 1024 * 1024, transcendentals=0),
        name="fold",
    )(*pieces)


def close_kernel(p_ref, o_ref):
    for h in range(4):
        total = p_ref[4 * h].astype(jnp.float32)
        for s in range(1, 4):
            total = total + p_ref[4 * h + s].astype(jnp.float32)
        o_ref[:, h * HD : (h + 1) * HD] = total[:, :HD]
        o_ref[:, (h + 4) * HD : (h + 5) * HD] = total[:, HD:]


def close(parts):
    return pl.pallas_call(
        close_kernel,
        out_shape=jax.ShapeDtypeStruct((32, 8 * HD), jnp.float32),
        in_specs=[VMEM],
        out_specs=VMEM,
        compiler_params=grant(4),
        name="close",
    )(parts)


def unpack_kernel(p_ref, after_ref, out_ref, grad_ref):
    for h in range(HEADS):
        out_ref[:, h * HD : (h + 1) * HD] = p_ref[h, 0:BLOCK]
        grad_ref[:, h * HD : (h + 1) * HD] = p_ref[h, BLOCK:]


def unpack(back, after):
    whole = jax.ShapeDtypeStruct((BLOCK, HEADS * HD), jnp.bfloat16)
    return pl.pallas_call(
        unpack_kernel,
        out_shape=(whole, whole),
        in_specs=[VMEM, ANY],
        out_specs=(VMEM, VMEM),
        compiler_params=grant(8),
        cost_estimate=pl.CostEstimate(flops=0, bytes_accessed=2 * 1024 * 1024, transcendentals=0),
        name="unpack",
    )(back, after)


def shift(v, axis, k):
    return lax.ppermute(v, axis, [(s, (s + k) % 4) for s in range(4)])


def swap(v):
    return lax.ppermute(v, "core", [(0, 1), (1, 0)])


def per_device(normed, queries, cotangent, lengths, balanced_slot, kv_weight):
    x, core, z, y = (lax.axis_index(name) for name in ("x", "core", "z", "y"))
    place = jnp.stack([z, y, x, core]).astype(jnp.int32)
    rows = pack(balanced_slot, queries[0], cotangent[0])
    *mine, keep, give = project(place, normed[0], kv_weight, rows)

    kv = [mine[0]] + [shift(mine[k], "z", k) for k in (1, 2, 3)]
    rows = lax.all_to_all(rows, CTX, 0, 0, tiled=True)
    tokens = join(keep, swap(give))
    kv = pile(kv, tokens)
    kv = [kv] + [shift(kv, "y", k) for k in (1, 2, 3)]
    left = shift(tokens, "z", 1)
    right = shift(tokens, "z", -1)
    across = shift(tokens, "z", 2)

    out, *dkv = attend(lengths, place, rows, kv)

    dkv = [dkv[0]] + [shift(dkv[k], "y", k) for k in (1, 2, 3)]
    back = lax.all_to_all(tie(out, dkv[1]), CTX, 0, 0, tiled=True)
    dkv = settle(dkv, (left, across, right))
    theirs = swap(dkv)

    pieces = weigh(place, dkv, theirs, (tokens, left, across, right))
    own = tie(dkv, pieces[1])
    pieces = [pieces[0]] + [shift(pieces[k], "x", k) for k in (1, 2, 3)]

    kv_grad = heads_side_by_side(place, [own[0]] + [shift(own[k], "z", -k) for k in (1, 2, 3)])
    input_grad = lax.dot_general(
        kv_grad, kv_weight, NT, preferred_element_type=jnp.float32
    ).astype(jnp.bfloat16)
    folded = tie(fold(pieces), back)
    weight_grad = close(lax.all_to_all(folded, CTX, 0, 0, tiled=True))
    attn_out, q_grad = unpack(back, folded)
    return (attn_out[None], q_grad[None], input_grad[None], weight_grad)


def solution(mesh):
    fine = Mesh(mesh.devices.reshape(4, 2, 4, 4), ("x", "core", "z", "y"))
    dp = ("x", "core")
    placed = (
        P(dp, CTX, None),
        P(dp, CTX, None),
        P(dp, CTX, None),
        P(dp, None),
        P(dp, CTX),
        P(),
    )
    return jax.shard_map(
        per_device,
        mesh=fine,
        in_specs=placed,
        out_specs=(
            P(dp, CTX, None),
            P(dp, CTX, None),
            P(dp, CTX, None),
            P(dp + CTX, None),
        ),
        check_vma=False,
    )
```
